32 devices in a mesh: tm: 8 (over z, y), head: 4 (over x, core).
Axes of the slice: x: 2, y: 2, z: 4, core: 2. Of those that a mesh axis runs over, the one named last changes fastest.
Arguments:
- feats_long: bfloat16 [8192, 80], P(('tm', 'head')), may hold values from -6 to 6
- feats_short: bfloat16 [49152, 80], P(('tm', 'head')), may hold values from -6 to 6
- long_length: int32 [1], replicated, may hold values from 1985 to 2048
- short_groups: int32 [32, 4], P(('tm', 'head')), may hold values from 1 to 6, 12 in all within a row
- freq_start: int32 [32], P(('tm', 'head')), may hold values from 0 to 53
- freq_width: int32 [32], P(('tm', 'head')), may hold values from 0 to 27
- time_start: int32 [32], P(('tm', 'head')), may hold values from 0 to 1436
- time_width: int32 [32], P(('tm', 'head')), may hold values from 0 to 100
- stem_weight: bfloat16 [512, 320], P(('tm', 'head')), may hold values from -0.3125 to 0.3125
- norm_gains: bfloat16 [512, 6], P(('tm', 'head')), may hold values from 0.25 to 1.75
- ffn1_up: bfloat16 [512, 2048], P(('tm', 'head')), may hold values from -0.25 to 0.25
- ffn1_down: bfloat16 [2048, 512], P(('tm', 'head')), may hold values from -0.125 to 0.125
- mixer_in: bfloat16 [512, 1024], P(('tm', 'head')), may hold values from -0.25 to 0.25
- mixer_out: bfloat16 [512, 512], P(('tm', 'head')), may hold values from -0.25 to 0.25
- mixer_log_rate: bfloat16 [512, 32], P(('tm', 'head')), may hold values from -12 to -2
- mixer_freq: bfloat16 [512, 32], P(('tm', 'head')), may hold values from -3.140625 to 3.140625
- mixer_coef: bfloat16 [512, 64], P(('tm', 'head')), may hold values from -1 to 1
- conv_taps: bfloat16 [512, 15], P(('tm', 'head')), may hold values from -1.5 to 1.5
- ffn2_up: bfloat16 [512, 2048], P(('tm', 'head')), may hold values from -0.25 to 0.25
- ffn2_down: bfloat16 [2048, 512], P(('tm', 'head')), may hold values from -0.125 to 0.125
- cotangent_long: bfloat16 [2048, 512], P(('tm', 'head')), may hold values from -6 to 6
- cotangent_short: bfloat16 [12288, 512], P(('tm', 'head')), may hold values from -6 to 6
Outputs:
- output_long: bfloat16 [2048, 512], P(('tm', 'head'))
- output_short: bfloat16 [12288, 512], P(('tm', 'head'))
- grad_feats_long: bfloat16 [8192, 80], P(('tm', 'head'))
- grad_feats_short: bfloat16 [49152, 80], P(('tm', 'head'))
- grad_stem_weight: float32 [512, 320], P(('tm', 'head'))
- grad_norm_gains: float32 [512, 6], P(('tm', 'head'))
- grad_ffn1_up: float32 [512, 2048], P(('tm', 'head'))
- grad_ffn1_down: float32 [2048, 512], P(('tm', 'head'))
- grad_mixer_in: float32 [512, 1024], P(('tm', 'head'))
- grad_mixer_out: float32 [512, 512], P(('tm', 'head'))
- grad_mixer_log_rate: float32 [512, 32], P(('tm', 'head'))
- grad_mixer_freq: float32 [512, 32], P(('tm', 'head'))
- grad_mixer_coef: float32 [512, 64], P(('tm', 'head'))
- grad_conv_taps: float32 [512, 15], P(('tm', 'head'))
- grad_ffn2_up: float32 [512, 2048], P(('tm', 'head'))
- grad_ffn2_down: float32 [2048, 512], P(('tm', 'head'))
The draws below stay inside these ranges and needn't reach their ends.
Inputs may be any that keep to these rules, and one draw needn't show every extreme that they name: `short_groups`: each row lists, in blocks of 32 frames, the lengths of the utterances that fill one device's 384 short frames in order; a row sums to 12.
All inputs are finite; a program needn't handle non-finite values.
Results may differ from the reference program's by a relative error of at most 0.018.
Values may be sent and summed in bfloat16 or wider, within the bound.
No kernel may reach another device: no remote copies, remote signals or barrier semaphores. Data moves between devices by JAX's collectives and lax.ppermute only.
A program may use at most 384 MiB of HBM per device.

```python
import math
import jax
import jax.numpy as jnp
import numpy as np
from jax import lax

D = 512
FF = 2048
NS = 32
MEL = 80
KC = 15
GROUP = 32
LONG_DEV = 64
SHORT_DEV = 384
UTT_DEV = 4
FMASK = 27
TMASK = 100
MOST = 192
LONG_FRAMES = 2048
SHORT_FRAMES = 12288
DEVICES = 32


def draw_mixer_log_rate(key, part):
    key = jax.random.fold_in(key, 17)
    slowest = math.log(0.3 / LONG_FRAMES)
    fastest = math.log(0.1)
    return jax.random.uniform(key, (D, NS), jnp.float32, slowest, fastest).astype(jnp.bfloat16)


def place_ends(array, own_key, smallest, top_value):
    index_at = [jax.random.randint(jax.random.fold_in(own_key, axis), (), 0, length) for axis, length in enumerate(array.shape)]
    main_axis = array.shape.index(max(array.shape))
    next_to = index_at[:main_axis] + [(index_at[main_axis] + 1) % array.shape[main_axis]] + index_at[main_axis + 1:]
    return array.at[tuple(index_at)].set(smallest).at[tuple(next_to)].set(top_value)


def block_scale(rng, extent, cuts, smallest, top_value):
    factor_of, own = 1.0, jax.random.fold_in(rng, 6)
    for position, blocks in cuts:
        steps = jnp.exp(jax.random.uniform(jax.random.fold_in(own, position), (blocks,), jnp.float32, smallest / len(cuts), top_value / len(cuts)))
        factor_of = factor_of * jnp.repeat(steps, extent[position] // blocks).reshape([-1 if axis == position else 1 for axis in range(len(extent))])
    return factor_of


def profile(number_of, total, bound, slope):
    portions = [(1 << 20) // math.isqrt(rank ** slope) + 1 for rank in range(2, number_of + 1)]
    rest, given = total - bound - (number_of - 1), [1] * (number_of - 1)
    while rest > 0:
        free = [i for i in range(number_of - 1) if given[i] < bound]
        whole, budget = sum([portions[i] for i in free]), rest
        for i in free:
            more = min(bound - given[i], max(1, budget * portions[i] // whole), rest)
            given[i] = given[i] + more
            rest = rest - more
    return np.array([bound] + given)


def ragged(stream_key, number_of, total, reach, skew):
    if number_of == 2:
        one = jax.random.randint(stream_key, (), max(1, total - reach), min(reach, total - 1) + 1)
        return jnp.stack([one, total - one])
    lengths = jnp.asarray(profile(number_of, total, reach, skew), jnp.int32)
    pairs = (number_of - 1) // 2
    source_of, receiver = lengths[1:1 + 2 * pairs:2], lengths[2:2 + 2 * pairs:2]
    room = jnp.minimum(source_of - 1, reach - receiver)
    moved = jax.random.randint(jax.random.fold_in(stream_key, 1), (pairs,), 0, 1 << 20) % (room + 1)
    lengths = lengths.at[1:1 + 2 * pairs:2].set(source_of - moved).at[2:2 + 2 * pairs:2].set(receiver + moved)
    return lengths[jax.random.permutation(jax.random.fold_in(stream_key, 2), number_of)]


def bell_draw(key, extent, scale, limit, split=(), dtype=jnp.bfloat16):
    array = jax.random.normal(key, extent, jnp.float32) * scale
    if len(split) > 0:
        array = block_scale(key, extent, split, -0.22, 0.18) * array
    return jnp.clip(array, min=-limit, max=limit).astype(dtype)


def setup_inputs(seed: int = 0) -> dict:
    splits = jax.random.split(jax.random.key(seed), 23)
    return {
        "feats_long": bell_draw(splits[0], (4 * LONG_FRAMES, MEL), 1.0, 6.0, ((0, 32),)),
        "feats_short": bell_draw(splits[1], (4 * SHORT_FRAMES, MEL), 1.0, 6.0, ((0, 32),)),
        "long_length": jax.random.randint(splits[2], (1,), LONG_FRAMES - LONG_DEV + 1, LONG_FRAMES + 1).astype(jnp.int32),
        "short_groups": jax.vmap(lambda own: ragged(own, UTT_DEV, SHORT_DEV // GROUP, MOST // GROUP, 2))(jax.random.split(splits[3], DEVICES)).reshape((DEVICES, UTT_DEV)).astype(jnp.int32),
        "freq_start": place_ends(jax.random.randint(splits[4], (DEVICES,), 0, MEL - FMASK + 1), jax.random.fold_in(splits[4], 1), 0, MEL - FMASK).astype(jnp.int32),
        "freq_width": place_ends(jax.random.randint(splits[5], (DEVICES,), 0, FMASK + 1), jax.random.fold_in(splits[5], 1), 0, FMASK).astype(jnp.int32),
        "time_start": place_ends(jax.random.randint(splits[6], (DEVICES,), 0, 4 * SHORT_DEV - TMASK + 1), jax.random.fold_in(splits[6], 1), 0, 4 * SHORT_DEV - TMASK).astype(jnp.int32),
        "time_width": place_ends(jax.random.randint(splits[7], (DEVICES,), 0, TMASK + 1), jax.random.fold_in(splits[7], 1), 0, TMASK).astype(jnp.int32),
        "stem_weight": bell_draw(splits[8], (D, 4 * MEL), (4 * MEL) ** -0.5, 0.3125, ((0, 32),)),
        "norm_gains": jnp.clip(1.0 + 0.15 * jax.random.normal(splits[9], (D, 6), jnp.float32), 0.25, 1.75).astype(jnp.bfloat16),
        "ffn1_up": bell_draw(splits[10], (D, FF), D ** -0.5, 0.25, ((0, 32),)),
        "ffn1_down": bell_draw(splits[11], (FF, D), FF ** -0.5, 0.125, ((0, 32),)),
        "mixer_in": bell_draw(splits[12], (D, 2 * D), D ** -0.5, 0.25, ((0, 32),)),
        "mixer_out": bell_draw(splits[13], (D, D), D ** -0.5, 0.25, ((0, 32),)),
        "mixer_log_rate": draw_mixer_log_rate(jax.random.fold_in(splits[22], 71), 0),
        "mixer_freq": jnp.clip(jax.random.uniform(splits[15], (D, NS), jnp.float32, -3.140625, 3.140625), -3.140625, 3.140625).astype(jnp.bfloat16),
        "mixer_coef": bell_draw(splits[16], (D, 2 * NS), NS ** -0.5, 1.0, ((0, 32),)),
        "conv_taps": bell_draw(splits[17], (D, KC), KC ** -0.5, 1.5, ((0, 32),)),
        "ffn2_up": bell_draw(splits[18], (D, FF), D ** -0.5, 0.25, ((0, 32),)),
        "ffn2_down": bell_draw(splits[19], (FF, D), FF ** -0.5, 0.125, ((0, 32),)),
        "cotangent_long": bell_draw(splits[20], (LONG_FRAMES, D), 1.0, 6.0, ((0, 32),)),
        "cotangent_short": bell_draw(splits[21], (SHORT_FRAMES, D), 1.0, 6.0, ((0, 32),)),
    }


highest = lax.Precision.HIGHEST

@jax.custom_vjp
def low(v):
    return lax.optimization_barrier(v.astype(jnp.bfloat16)).astype(jnp.float32)

@jax.custom_vjp
def low_back(v):
    return v

def low_keep(v):
    return (low(v), None)

def low_pass(kept, grad):
    return (grad,)

def back_keep(v):
    return (v, None)

def back_low(kept, grad):
    return (low(grad),)
low.defvjp(low_keep, low_pass)
low_back.defvjp(back_keep, back_low)

def matmul(first_op, second_op):
    return jnp.dot(first_op, second_op, precision=highest, preferred_element_type=jnp.float32)

def norm_rows(values, gain_row):
    centred = values - lax.optimization_barrier(jnp.mean(values, axis=-1, keepdims=True))
    variance = lax.optimization_barrier(jnp.mean(centred * centred, axis=-1, keepdims=True))
    return centred * lax.rsqrt(variance + 1e-05) * gain_row

def ssm_tables(log_rate, freq_values, coef_values, block_width):
    rate_values = jnp.exp(log_rate)
    step_index = jnp.arange(block_width + 1).astype(jnp.float32)
    decays = jnp.exp(-rate_values[:, :, None] * step_index)
    phases = freq_values[:, :, None] * step_index
    scales = jnp.sqrt(2.0 * rate_values)
    states = log_rate.shape[1]
    return (decays * jnp.cos(phases), decays * jnp.sin(phases), scales * coef_values[:, :states], scales * coef_values[:, states:])

def chain_step(previous, current):
    return (current[0] * previous[0] - current[1] * previous[1], current[0] * previous[1] + current[1] * previous[0], current[0] * previous[2] - current[1] * previous[3] + current[2], current[0] * previous[3] + current[1] * previous[2] + current[3])

def group_scan(source, keep_flags, tables, start_real, start_imaginary):
    power_real, power_imaginary, weight_real, weight_imaginary = tables
    block_width = power_real.shape[2] - 1
    row_count, channels = source.shape
    block_count = row_count // block_width
    kernel = lax.optimization_barrier(jnp.sum(weight_real[:, :, None] * power_real[:, :, :block_width] - weight_imaginary[:, :, None] * power_imaginary[:, :, :block_width], axis=1))
    lag_index = jnp.arange(block_width)[:, None] - jnp.arange(block_width)[None, :]
    toeplitz = jnp.where(lag_index[None] >= 0, kernel[:, jnp.clip(lag_index, 0, block_width - 1)], 0.0)
    blocks = source.reshape(block_count, block_width, channels)
    within = jnp.einsum('cts,jsc->jtc', toeplitz, blocks, precision=highest)
    flip_real = power_real[:, :, :block_width][:, :, ::-1]
    flip_imaginary = power_imaginary[:, :, :block_width][:, :, ::-1]
    added_real = jnp.einsum('jsc,cns->jcn', blocks, flip_real, precision=highest)
    added_imaginary = jnp.einsum('jsc,cns->jcn', blocks, flip_imaginary, precision=highest)
    scale_real = keep_flags[:, None, None] * power_real[None, :, :, block_width]
    scale_imaginary = keep_flags[:, None, None] * power_imaginary[None, :, :, block_width]
    totals = lax.associative_scan(chain_step, (scale_real, scale_imaginary, added_real, added_imaginary), axis=0)
    state_real = totals[2] + totals[0] * start_real - totals[1] * start_imaginary
    state_imaginary = totals[3] + totals[0] * start_imaginary + totals[1] * start_real
    before_real = jnp.concatenate([start_real[None], state_real[:-1]], axis=0)
    before_imaginary = jnp.concatenate([start_imaginary[None], state_imaginary[:-1]], axis=0)
    lead_real = weight_real[:, :, None] * power_real[:, :, 1:] - weight_imaginary[:, :, None] * power_imaginary[:, :, 1:]
    lead_imaginary = weight_real[:, :, None] * power_imaginary[:, :, 1:] + weight_imaginary[:, :, None] * power_real[:, :, 1:]
    carried = jnp.einsum('jcn,cnt->jtc', before_real, lead_real, precision=highest) - jnp.einsum('jcn,cnt->jtc', before_imaginary, lead_imaginary, precision=highest)
    mixed_out = within + carried * keep_flags[:, None, None]
    return (mixed_out.reshape(row_count, channels), state_real[-1], state_imaginary[-1])

def group_keep(utter_ids, block_width):
    firsts = utter_ids[::block_width]
    last_ids = jnp.concatenate([jnp.full((1,), -1, jnp.int32), utter_ids[block_width - 1::block_width][:-1].astype(jnp.int32)])
    return (firsts.astype(jnp.int32) == last_ids).astype(jnp.float32)

def rim_mask(utter_ids, half_span):
    row_count = utter_ids.shape[0]
    padded = jnp.pad(utter_ids.astype(jnp.int32), (half_span, half_span), constant_values=-1)
    return jnp.stack([(padded[offset:offset + row_count] == utter_ids.astype(jnp.int32)).astype(jnp.float32) for offset in range(2 * half_span + 1)], axis=1)

def depthwise(padded, same_mask, conv_taps):
    row_count = same_mask.shape[0]
    summed = jnp.zeros((row_count, padded.shape[1]), jnp.float32)
    for offset in range(conv_taps.shape[1]):
        summed = summed + padded[offset:offset + row_count] * same_mask[:, offset:offset + 1] * conv_taps[:, offset]
    return summed

def feed_forward(residual, gain_row, weight_up, weight_down):
    normed = low(norm_rows(residual, gain_row))
    hidden = low_back(matmul(normed, weight_up))
    active = low(jax.nn.silu(hidden))
    return low_back(matmul(active, weight_down))

def layer(stacked, valid_rows, utter_ids, params):
    stem_weight, norm_gains, ffn1_up, ffn1_down, mixer_in, mixer_out, log_rate, freq_values, coef_values, conv_taps, ffn2_up, ffn2_down = params
    features = norm_gains.shape[0]
    residual = low_back(matmul(stacked, stem_weight.T))
    residual1 = residual + 0.5 * feed_forward(residual, norm_gains[:, 0], ffn1_up, ffn1_down)
    normed = low(norm_rows(residual1, norm_gains[:, 1]))
    projected = low_back(matmul(normed, mixer_in))
    inputs_b = low(projected[:, :features])
    gates = projected[:, features:]
    source = low_back(inputs_b * valid_rows[:, None])
    tables = ssm_tables(log_rate, freq_values, coef_values, GROUP)
    zero_state = jnp.zeros(log_rate.shape, jnp.float32)
    mixed_out = group_scan(source, group_keep(utter_ids, GROUP), tables, zero_state, zero_state)[0]
    mixed_out = low(low_back(mixed_out))
    joined = mixed_out + norm_gains[:, 5] * inputs_b
    gated = low(joined * jax.nn.silu(gates))
    residual2 = residual1 + low_back(matmul(gated, mixer_out))
    normed3 = low(norm_rows(residual2, norm_gains[:, 2]))
    half_span = conv_taps.shape[1] // 2
    padded = jnp.pad(normed3 * valid_rows[:, None], ((half_span, half_span), (0, 0)))
    conv_out = low_back(depthwise(padded, rim_mask(utter_ids, half_span), conv_taps))
    residual3 = residual2 + jax.nn.silu(conv_out)
    residual4 = residual3 + 0.5 * feed_forward(residual3, norm_gains[:, 3], ffn2_up, ffn2_down)
    return norm_rows(residual4, norm_gains[:, 4])

def reference(feats_long, feats_short, long_length, short_groups, freq_start, freq_width, time_start, time_width, stem_weight, norm_gains, ffn1_up, ffn1_down, mixer_in, mixer_out, mixer_log_rate, mixer_freq, mixer_coef, conv_taps, ffn2_up, ffn2_down, cotangent_long, cotangent_short):
    weights = tuple((weight.astype(jnp.float32) for weight in (stem_weight, norm_gains, ffn1_up, ffn1_down, mixer_in, mixer_out, mixer_log_rate, mixer_freq, mixer_coef, conv_taps, ffn2_up, ffn2_down)))
    mel_index = jnp.arange(MEL)
    mel_band = (mel_index[None, :] >= freq_start[:, None]) & (mel_index[None, :] < (freq_start + freq_width)[:, None])
    freq_keep = 1.0 - mel_band.astype(jnp.float32)
    row_index = jnp.arange(4 * SHORT_DEV)
    time_blank = (row_index[None, :] >= time_start[:, None]) & (row_index[None, :] < (time_start + time_width)[:, None])
    time_keep = 1.0 - time_blank.astype(jnp.float32)
    valid_long = (jnp.arange(LONG_FRAMES) < long_length[0]).astype(jnp.float32)
    starts = jnp.cumsum(short_groups, axis=1) - short_groups
    group_of = jnp.arange(SHORT_DEV) // GROUP
    short_ids = (lax.optimization_barrier(jnp.sum((starts[:, None, :] <= group_of[None, :, None]).astype(jnp.int32), axis=2)) - 1).astype(jnp.int32)
    long_ids = jnp.zeros((LONG_FRAMES,), jnp.int32)
    ones_short = jnp.ones((SHORT_DEV,), jnp.float32)

    def forward(long_feats, short_feats, params):
        stacked_long = (long_feats.reshape(DEVICES, 4 * LONG_DEV, MEL) * freq_keep[:, None, :]).reshape(LONG_FRAMES, 4 * MEL)
        out_long = jax.checkpoint(layer)(stacked_long, valid_long, long_ids, params)

        def short_block(pieces):
            feats_device, freq_device, time_device, ids_device = pieces
            stacked = (feats_device * freq_device[None, :] * time_device[:, None]).reshape(SHORT_DEV, 4 * MEL)
            return layer(stacked, ones_short, ids_device, params)
        out_short = lax.map(jax.checkpoint(short_block), (short_feats.reshape(DEVICES, 4 * SHORT_DEV, MEL), freq_keep, time_keep, short_ids))
        return (out_long, out_short.reshape(DEVICES * SHORT_DEV, -1))
    outputs, pullback = jax.vjp(forward, feats_long.astype(jnp.float32), feats_short.astype(jnp.float32), weights)
    grad_long, grad_short, grads = pullback((cotangent_long.astype(jnp.float32), cotangent_short.astype(jnp.float32)))
    return (outputs[0].astype(jnp.bfloat16), outputs[1].astype(jnp.bfloat16), grad_long.astype(jnp.bfloat16), grad_short.astype(jnp.bfloat16), grads[0], grads[1], grads[2], grads[3], grads[4], grads[5], grads[6], grads[7], grads[8], grads[9], grads[10], grads[11])
```

```python
from functools import partial

import jax
import jax.numpy as jnp
from jax import lax
from jax.experimental import pallas as pl
from jax.experimental.pallas import tpu as pltpu
from jax.sharding import PartitionSpec as P

GROUP = 32
LAGS = 192
TILE = 8
LANES = 256
SMALL_ROWS = 32
AXES = ("tm", "head")

f32 = jnp.float32
bf16 = jnp.bfloat16


def bits_of(axis):
    return (lax.axis_size(axis) - 1).bit_length()


def grid_of():
    tm, head = lax.axis_size("tm"), lax.axis_size("head")
    y = 1 << ((bits_of("tm") - 1) // 2)
    return tm // y, y, head // 2, 2


def places():
    _, y, x, _ = grid_of()
    names = [("tm", b) for b in reversed(range(y.bit_length() - 1))]
    return names + [("head", b) for b in reversed(range(bits_of("head")))]


def bit_order(first):
    heads = [n for n in places() if n[0] == "head" and n[1] > 0]
    tms = [n for n in places() if n[0] == "tm"]
    return heads + tms if first == "x" else tms + heads


def my_bit(name):
    return (lax.axis_index(name[0]) >> name[1]) & 1


def swap(value, name):
    axis, bit = name
    return lax.ppermute(value, axis, [(i, i ^ (1 << bit)) for i in range(lax.axis_size(axis))])


def send_along_z(value, hops):
    z, y, _, _ = grid_of()
    pairs = [(i, (i // y + hops) % z * y + i % y) for i in range(z * y)]
    return lax.ppermute(value, "tm", pairs)


def my_z():
    return lax.axis_index("tm") // grid_of()[1]


def joined_at(dim, mine, other, place):
    shape = mine.shape[:dim] + (2,) + mine.shape[dim:]
    index = lax.broadcasted_iota(jnp.int32, shape, dim)
    wide = lambda v: jnp.broadcast_to(jnp.expand_dims(v, dim), shape)
    return jnp.where(index == place, wide(mine), wide(other))


def tied(first, then):
    return lax.optimization_barrier((first, then))


def stacked_along_z(got):
    z = len(got)
    index = lax.broadcasted_iota(jnp.int32, (z,) + got[0].shape, 0)
    held = jnp.broadcast_to(got[0], index.shape)
    for hops in range(1, z):
        held = jnp.where(index == (my_z() - hops) % z, got[hops], held)
    return held


def pick(array, index):
    starts = [jnp.int32(0) if i is None else i for i in index]
    sizes = [n if i is None else 1 for n, i in zip(array.shape, index)]
    kept = [n for n, i in zip(array.shape, index) if i is None]
    tail = list(array.shape[len(index) :])
    starts += [jnp.int32(0)] * len(tail)
    return lax.dynamic_slice(array, starts, sizes + tail).reshape(kept + tail).astype(f32)


def settle(fold, values):
    newest, values = tied([terms[-1][0] for terms in fold.terms], values)
    for terms, array in zip(fold.terms, newest):
        terms[-1] = (array, terms[-1][1])
    return values


def all_bits():
    bits = [("tm", b) for b in reversed(range(bits_of("tm")))]
    return bits + [("head", b) for b in reversed(range(bits_of("head")))]


class Folding:
    last = None

    def __init__(self, grads, join=None):
        names = all_bits()
        self.high = [n for n in names if n[0] == "tm" and n not in places()]
        self.terms = [[(g.reshape((2,) * len(names) + g.shape[1:]), names)] for g in grads]
        firsts = "y" if len(grads) == 1 else "xy"
        self.todo = [[("head", 0)] + bit_order(first) for first in firsts]
        if join is None:
            self.todo = [todo + self.high[::-1] for todo in self.todo]
        self.fixed = [{} for _ in grads]
        self.join = join
        self.done = False

    def total(self, color, fixed):
        value = None
        for array, names in self.terms[color]:
            piece = pick(array, [fixed.get(name) for name in names])
            value = piece if value is None else value + piece
        return value

    def at_z(self, color, z):
        bits = {name: (z >> place) & 1 for place, name in enumerate(self.high[::-1])}
        return self.total(color, {**self.fixed[color], **bits})

    def load(self):
        if Folding.last is not None:
            newest = [terms[-1][0] for terms in self.terms]
            newest = tied(Folding.last, newest)[1]
            for terms, array in zip(self.terms, newest):
                terms[-1] = (array, terms[-1][1])
        colors = range(len(self.terms))
        values = []
        if self.todo[0]:
            for color in colors:
                name = self.todo[color][0]
                fixed = {**self.fixed[color], name: 1 - my_bit(name)}
                values.append(self.total(color, fixed).astype(bf16))
        elif self.join is not None:
            z = grid_of()[0]
            for hops in range(1, z):
                parts = [self.at_z(c, (my_z() + hops) % z).astype(bf16) for c in colors]
                values.append(jnp.concatenate(parts, axis=self.join))
        Folding.last = values or None
        return values

    def send(self, values):
        if self.todo[0]:
            for color, value in enumerate(values):
                name = self.todo[color].pop(0)
                got = swap(value, name)
                self.fixed[color][name] = my_bit(name)
                left = [n for n in all_bits() if n not in self.fixed[color]]
                self.terms[color].append((got, left))
        else:
            self.got = [send_along_z(v, hops + 1).astype(f32) for hops, v in enumerate(values)]
            self.done = True
        if self.join is None:
            self.done = not self.todo[0]

    def result(self):
        while not self.done:
            advance([self])
        if self.join is None:
            return [self.total(c, self.fixed[c]) for c in range(len(self.terms))]
        sums = [self.at_z(c, my_z()) for c in range(len(self.terms))]
        if len(sums) == 1:
            return [sums[0] + sum(self.got)]
        cut = sums[0].shape[self.join]
        for got in self.got:
            pieces = (got[:cut], got[cut:]) if self.join == 0 else (got[:, :cut], got[:, cut:])
            sums = [a + b for a, b in zip(sums, pieces)]
        return sums


def advance(folds, values=()):
    for fold in folds:
        if not fold.done:
            load, values = tied(fold.load(), values)
            fold.send(load)
    return values


def exchange(rows):
    return lax.all_to_all(rows, AXES, split_axis=0, concat_axis=0, tiled=True)


def edges(x, width):
    size = lax.axis_size("tm") * lax.axis_size("head")
    up = [(i, i + 1) for i in range(size - 1)]
    down = [(j, i) for i, j in up]
    before = lax.ppermute(x[x.shape[0] - width :], AXES, up)
    after = lax.ppermute(x[:width], AXES, down)
    return before, after


def row_dot(a, b):
    return jnp.dot(a, b, preferred_element_type=f32)


def inner_dot(a, b):
    return lax.dot_general(a, b, (((0,), (0,)), ((), ())), preferred_element_type=f32)


def outer_dot(a, b):
    return lax.dot_general(a, b, (((1,), (1,)), ((), ())), preferred_element_type=f32)


def norm(values):
    centred = values - jnp.mean(values, axis=-1, keepdims=True)
    scale = lax.rsqrt(jnp.mean(centred * centred, axis=-1, keepdims=True) + 1e-05)
    return centred * scale, scale


def norm_back(grad, gain, hat, scale):
    e = grad * gain
    back = e - jnp.mean(e, axis=-1, keepdims=True)
    back = (back - hat * jnp.mean(e * hat, axis=-1, keepdims=True)) * scale
    return back, jnp.sum(grad * hat, axis=0)


def silu_slope(values):
    logistic = jax.nn.sigmoid(values)
    return logistic * (1.0 + values * (1.0 - logistic))


def ffn_forward(residual, gain, up, down):
    hat, scale = norm(residual)
    normed = (hat * gain).astype(bf16)
    hidden = jnp.concatenate([row_dot(normed, part) for part in up], axis=1)
    active = jax.nn.silu(hidden).astype(bf16)
    return row_dot(active, down), (normed, hidden, active, hat, scale)


def column_blocks(x, width):
    return [x[:, i : i + width] for i in range(0, x.shape[1], width)]


def back_through(grad, parts):
    blocks = column_blocks(grad, grad.shape[1] // len(parts))
    return sum(outer_dot(block, part) for block, part in zip(blocks, parts))


def hidden_grad(grad_b, kept, down):
    return (outer_dot(grad_b, down) * silu_slope(kept[1])).astype(bf16)


def utterance_edges(groups, lead, blocks, block):
    first = jnp.int32(0)
    after = jnp.int32(lead)
    begin = jnp.int32(lead)
    for u in range(groups.shape[1]):
        end = begin + groups[0, u]
        inside = block >= begin
        first = jnp.where(inside, begin, first)
        after = jnp.where(inside, end, after)
        begin = end
    return first, after


def lag_tile(table, shift, tile):
    if isinstance(tile, int):
        return table[shift, tile * TILE : (tile + 1) * TILE, :]
    return table[shift, pl.ds(pl.multiple_of(tile * TILE, TILE), TILE), :]


def mix_forward_kernel(lead, groups, source, taps, out, rows_f, padded, table):
    blocks = source.shape[0] // GROUP
    tiles = GROUP // TILE
    rows_f[...] = source[...].astype(f32)
    padded[0:TILE, :] = jnp.zeros((TILE, padded.shape[1]), f32)
    padded[TILE:, :] = taps[...]
    for q in range(TILE):
        table[q] = padded[TILE - q : TILE - q + LAGS, :]

    def tile_of(ref, block, i):
        return ref[pl.ds(pl.multiple_of(block * GROUP + i * TILE, TILE), TILE), :]

    def one(block, carry):
        first, _ = utterance_edges(groups, lead, blocks, block)
        sums = [jnp.zeros((TILE, rows_f.shape[1]), f32) for _ in range(tiles)]
        own = [tile_of(rows_f, block, j) for j in range(tiles)]
        for q in range(TILE):
            lags = [lag_tile(table, q, d) for d in range(tiles)]
            for j in range(tiles):
                row = own[j][q : q + 1, :]
                for i in range(j, tiles):
                    sums[i] = sums[i] + lags[i - j] * row

        def pair(other, sums):
            sums = list(sums)
            base = (block - other) * tiles
            own = [tile_of(rows_f, other, j) for j in range(tiles)]
            for q in range(TILE):
                lags = {d: lag_tile(table, q, base + d) for d in range(1 - tiles, tiles)}
                for j in range(tiles):
                    row = own[j][q : q + 1, :]
                    for i in range(tiles):
                        sums[i] = sums[i] + lags[i - j] * row
            return tuple(sums)

        sums = lax.fori_loop(first, block, pair, tuple(sums))
        for i in range(tiles):
            out[pl.ds(pl.multiple_of(block * GROUP + i * TILE, TILE), TILE), :] = sums[i]
        return carry

    lax.fori_loop(0, blocks, one, 0)


def mix_backward_kernel(
    lead, groups, grad, source, taps_flipped, out, grad_taps, grad_f, rows_f, padded, table, sums_q
):
    blocks = source.shape[0] // GROUP
    tiles = GROUP // TILE
    top = LAGS // TILE - 1
    grad_f[...] = grad[...].astype(f32)
    rows_f[...] = source[...].astype(f32)
    padded[0:LAGS, :] = taps_flipped[...]
    padded[LAGS:, :] = jnp.zeros((TILE, padded.shape[1]), f32)
    for q in range(TILE):
        table[q] = padded[q : q + LAGS, :]
        sums_q[q] = jnp.zeros(sums_q.shape[1:], f32)

    def tile_of(ref, block, i):
        return ref[pl.ds(pl.multiple_of(block * GROUP + i * TILE, TILE), TILE), :]

    def add_to(q, tile, value):
        if isinstance(tile, int):
            place = slice(tile * TILE, (tile + 1) * TILE)
        else:
            place = pl.ds(pl.multiple_of(tile * TILE, TILE), TILE)
        sums_q[q, place, :] = sums_q[q, place, :] + value

    def one(block, carry):
        _, after = utterance_edges(groups, lead, blocks, block)
        sums = [jnp.zeros((TILE, rows_f.shape[1]), f32) for _ in range(tiles)]
        own = [tile_of(rows_f, block, j) for j in range(tiles)]
        here = [tile_of(grad_f, block, i) for i in range(tiles)]
        for q in range(TILE):
            lags = [lag_tile(table, TILE - 1 - q, top - d) for d in range(tiles)]
            for i in range(tiles):
                row = here[i][q : q + 1, :]
                for j in range(i + 1):
                    sums[j] = sums[j] + lags[i - j] * row
            rows = [own[j][q : q + 1, :] for j in range(tiles)]
            for d in range(tiles):
                total = here[d] * rows[0]
                for j in range(1, tiles - d):
                    total = total + here[d + j] * rows[j]
                add_to(q, d, total)

        def pair(other, sums):
            sums = list(sums)
            base = (other - block) * tiles
            here = [tile_of(grad_f, other, i) for i in range(tiles)]
            for q in range(TILE):
                lags = {
                    d: lag_tile(table, TILE - 1 - q, top - base - d)
                    for d in range(1 - tiles, tiles)
                }
                for i in range(tiles):
                    row = here[i][q : q + 1, :]
                    for j in range(tiles):
                        sums[j] = sums[j] + lags[i - j] * row
                rows = [own[j][q : q + 1, :] for j in range(tiles)]
                for d in range(1 - tiles, tiles):
                    total = None
                    for j in range(tiles):
                        if 0 <= j + d < tiles:
                            term = here[j + d] * rows[j]
                            total = term if total is None else total + term
                    add_to(q, base + d, total)
            return tuple(sums)

        sums = lax.fori_loop(block + 1, after, pair, tuple(sums))
        for j in range(tiles):
            out[pl.ds(pl.multiple_of(block * GROUP + j * TILE, TILE), TILE), :] = sums[j]
        return carry

    lax.fori_loop(0, blocks, one, 0)
    total = sums_q[0, 0:LAGS, :]
    for q in range(1, TILE):
        total = total + sums_q[q, q : q + LAGS, :]
    grad_taps[...] = total


def mixer_params():
    return pltpu.CompilerParams(vmem_limit_bytes=40 * 1024 * 1024)


def mix_forward(lead, groups, source, taps):
    rows, features = source.shape
    lanes = min(LANES, features)
    column = lambda count: pl.BlockSpec((count, lanes), lambda i: (0, i))
    return pl.pallas_call(
        partial(mix_forward_kernel, lead),
        out_shape=jax.ShapeDtypeStruct((rows, features), f32),
        grid=(features // lanes,),
        in_specs=[pl.BlockSpec(memory_space=pltpu.SMEM), column(rows), column(LAGS)],
        out_specs=column(rows),
        scratch_shapes=[
            pltpu.VMEM((rows, lanes), f32),
            pltpu.VMEM((LAGS + TILE, lanes), f32),
            pltpu.VMEM((TILE, LAGS, lanes), f32),
        ],
        compiler_params=mixer_params(),
        cost_estimate=pl.CostEstimate(
            flops=30000 * rows * features, bytes_accessed=rows * features * 8, transcendentals=0
        ),
        name="mix_forward",
    )(groups, source, taps)


def mix_backward(lead, groups, grad, source, taps_flipped, begin, width, into=None):
    rows, features = source.shape
    column = lambda count: pl.BlockSpec((count, width), lambda i: (0, begin))
    kept = [] if into is None else list(into)
    kernel = partial(mix_backward_kernel, lead)

    def body(*refs):
        kernel(*refs[:4], *refs[4 + len(kept) :])

    return pl.pallas_call(
        body,
        out_shape=(
            jax.ShapeDtypeStruct((rows, features), f32),
            jax.ShapeDtypeStruct((LAGS, features), f32),
        ),
        grid=(1,),
        in_specs=[
            pl.BlockSpec(memory_space=pltpu.SMEM),
            column(rows),
            column(rows),
            column(LAGS),
        ]
        + [pl.BlockSpec(memory_space=pl.ANY)] * len(kept),
        out_specs=(column(rows), column(LAGS)),
        scratch_shapes=[
            pltpu.VMEM((rows, width), f32),
            pltpu.VMEM((rows, width), f32),
            pltpu.VMEM((LAGS + TILE, width), f32),
            pltpu.VMEM((TILE, LAGS, width), f32),
            pltpu.VMEM((TILE, LAGS + TILE, width), f32),
        ],
        input_output_aliases={4 + i: i for i in range(len(kept))},
        compiler_params=mixer_params(),
        cost_estimate=pl.CostEstimate(
            flops=10000 * rows * width, bytes_accessed=rows * width * 8, transcendentals=0
        ),
        name="mix_backward",
    )(groups, grad, source, taps_flipped, *kept)


def fill_window(window, rows, before, after, lead, groups, block, blocks):
    first, stop = utterance_edges(groups, lead, blocks, block)
    place = lambda start, count: pl.ds(pl.multiple_of(start, 2 * TILE), count)
    window[TILE : TILE + GROUP, :] = rows[place(block * GROUP, GROUP), :].astype(f32)
    empty = jnp.zeros((TILE, window.shape[1]), f32)
    start = jnp.maximum(block * GROUP - 2 * TILE, 0)
    left = rows[place(start, 2 * TILE), :].astype(f32)[TILE:]
    left = jnp.where(block == 0, before[...].astype(f32), left)
    window[0:TILE, :] = jnp.where((block == 0) | (block > first), left, empty)
    start = jnp.minimum((block + 1) * GROUP, (blocks - 1) * GROUP)
    right = rows[place(start, 2 * TILE), :].astype(f32)[:TILE]
    right = jnp.where(block == lead - 1, after[...].astype(f32), right)
    keep = (block == lead - 1) | (block + 1 < stop)
    window[TILE + GROUP :, :] = jnp.where(keep, right, empty)


def conv_forward_kernel(lead, count, groups, rows, before, after, taps, out, window):
    blocks = rows.shape[0] // GROUP
    shift = TILE - count // 2

    def one(block, carry):
        fill_window(window, rows, before, after, lead, groups, block, blocks)
        total = None
        for k in range(count):
            term = window[shift + k : shift + k + GROUP, :] * taps[k : k + 1, :]
            total = term if total is None else total + term
        out[pl.ds(pl.multiple_of(block * GROUP, GROUP), GROUP), :] = total
        return carry

    lax.fori_loop(0, blocks, one, 0)


def conv_backward_kernel(
    lead, count, groups, grads, g_before, g_after, rows, before, after, taps, out, grad_taps,
    g_window, window, sums,
):
    blocks = rows.shape[0] // GROUP
    shift = TILE - count // 2
    sums[...] = jnp.zeros(sums.shape, f32)

    def one(block, carry):
        fill_window(g_window, grads, g_before, g_after, lead, groups, block, blocks)
        fill_window(window, rows, before, after, lead, groups, block, blocks)
        here = g_window[TILE : TILE + GROUP, :]
        total = None
        for k in range(count):
            lag = shift + count - 1 - k
            term = g_window[lag : lag + GROUP, :] * taps[k : k + 1, :]
            total = term if total is None else total + term
            product = here * window[shift + k : shift + k + GROUP, :]
            part = product[0:TILE]
            for i in range(TILE, GROUP, TILE):
                part = part + product[i : i + TILE]
            sums[k] = sums[k] + part
        out[pl.ds(pl.multiple_of(block * GROUP, GROUP), GROUP), :] = total
        return carry

    lax.fori_loop(0, blocks, one, 0)
    below = grad_taps.shape[0] - TILE - count
    grad_taps[...] = jnp.concatenate(
        [jnp.zeros((TILE, grad_taps.shape[1]), f32)]
        + [jnp.sum(sums[k], axis=0, keepdims=True) for k in range(count)]
        + [jnp.zeros((below, grad_taps.shape[1]), f32)],
        axis=0,
    )


def conv_call(kernel, lead, groups, arrays, outs, scratch, name):
    lanes = min(LANES, arrays[0].shape[1])
    column = lambda count: pl.BlockSpec((count, lanes), lambda i: (0, i))
    rows, features = arrays[0].shape
    return pl.pallas_call(
        kernel,
        out_shape=tuple(jax.ShapeDtypeStruct((n, features), f32) for n in outs),
        grid=(features // lanes,),
        in_specs=[pl.BlockSpec(memory_space=pltpu.SMEM)] + [column(a.shape[0]) for a in arrays],
        out_specs=tuple(column(n) for n in outs),
        scratch_shapes=[pltpu.VMEM(shape + (lanes,), f32) for shape in scratch],
        compiler_params=mixer_params(),
        cost_estimate=pl.CostEstimate(
            flops=4000 * rows * features, bytes_accessed=rows * features * 8, transcendentals=0
        ),
        name=name,
    )(groups, *arrays)


def conv_forward(lead, count, groups, rows, rim, taps):
    return conv_call(
        partial(conv_forward_kernel, lead, count),
        lead,
        groups,
        [rows, *rim, taps],
        [rows.shape[0]],
        [(GROUP + 2 * TILE,)],
        "conv_forward",
    )[0]


def conv_backward(lead, count, groups, grads, g_rim, rows, rim, taps):
    return conv_call(
        partial(conv_backward_kernel, lead, count),
        lead,
        groups,
        [grads, *g_rim, rows, *rim, taps],
        [rows.shape[0], SMALL_ROWS],
        [(GROUP + 2 * TILE,), (GROUP + 2 * TILE,), (count, TILE)],
        "conv_backward",
    )


def stack_rows(pieces, lanes):
    pieces = list(pieces)
    if any(p.shape[0] % 16 for p in pieces):
        fill = lambda p: jnp.pad(p, ((0, 0), (0, lanes - p.shape[1])))
        blocks = [b for p in pieces for b in (column_blocks(p, lanes) if p.shape[1] > lanes else [p])]
        return jnp.concatenate([fill(b) for b in blocks], axis=0)
    total = sum(p.shape[0] * -(-p.shape[1] // lanes) for p in pieces)

    def kernel(*refs):
        out, row = refs[-1], 0
        for ref in refs[:-1]:
            count, width = ref.shape
            for begin in range(0, width, lanes):
                here = min(lanes, width - begin)
                if here < lanes:
                    out[row : row + count, :] = jnp.zeros((count, lanes), out.dtype)
                out[row : row + count, 0:here] = ref[:, begin : begin + here]
                row += count

    return pl.pallas_call(
        kernel,
        out_shape=jax.ShapeDtypeStruct((total, lanes), pieces[0].dtype),
        in_specs=[pl.BlockSpec(memory_space=pltpu.VMEM)] * len(pieces),
        out_specs=pl.BlockSpec(memory_space=pltpu.VMEM),
        compiler_params=mixer_params(),
        name="stack_rows",
    )(*pieces)


def cmul(a, b):
    return (a[0] * b[0] - a[1] * b[1], a[0] * b[1] + a[1] * b[0])


def powers(rate, freq, steps):
    decay = jnp.exp(-rate * steps)
    return decay * jnp.cos(freq * steps), decay * jnp.sin(freq * steps)


def shifted(x, count):
    pad = jnp.zeros((abs(count),) + x.shape[1:], x.dtype)
    if count > 0:
        return jnp.concatenate([pad, x[:-count]], axis=0)
    return jnp.concatenate([x[-count:], pad], axis=0)


def chunk_scan(values, decay, sign):
    count = values[0].shape[0]
    hop = 1
    while hop < count:
        moved = tuple(shifted(v, sign * hop) for v in values)
        added = cmul(decay, moved)
        values = (values[0] + added[0], values[1] + added[1])
        decay = cmul(decay, decay)
        hop *= 2
    return values


def long_tables(log_rate, freq, coef, chunk):
    channels, states = log_rate.shape
    lanes = channels * states
    rate = jnp.exp(log_rate).reshape(1, lanes)
    freq = freq.reshape(1, lanes)
    scale = jnp.sqrt(2.0 * rate)
    weight = (
        scale * coef[:, :states].reshape(1, lanes),
        scale * coef[:, states:].reshape(1, lanes),
    )
    steps = jnp.arange(chunk + 1).astype(f32)[:, None]
    power = powers(rate, freq, steps)
    mask = jnp.arange(channels)[:, None] == (jnp.arange(lanes) // states)[None, :]
    mask = mask.astype(f32)[:, None, :]

    def spread(pair):
        wide = [(mask * part[None]).reshape(channels * chunk, lanes) for part in pair]
        return jnp.concatenate(wide, axis=1).astype(bf16)

    ages = tuple(p[:chunk][::-1] for p in power)
    leads = tuple(p[1:] for p in power)
    weighted = lambda pair: cmul(weight, pair)
    signed = lambda pair: (pair[0], -pair[1])
    return {
        "ages": spread(ages),
        "ages_slope": spread(tuple(a * steps[:chunk][::-1] for a in ages)),
        "leads": spread(leads),
        "leads_slope": spread(tuple(a * steps[1:] for a in leads)),
        "read": spread(signed(weighted(leads))),
        "read_back": spread(signed(weighted(ages))),
        "decay": powers(rate, freq, jnp.float32(chunk)),
        "rate": rate,
        "scale": scale,
        "weight": weight,
    }


def halves(x):
    lanes = x.shape[1] // 2
    return x[:, :lanes], x[:, lanes:]


def long_forward(rows, tables):
    added = halves(row_dot(rows, tables["ages"]))
    state = chunk_scan(added, tables["decay"], 1)
    before = tuple(shifted(v, 1) for v in state)
    carried = outer_dot(jnp.concatenate(before, axis=1).astype(bf16), tables["read"])
    return carried, before


def long_backward(grads, tables):
    read = halves(row_dot(grads, tables["leads"]))
    future = chunk_scan(read, tables["decay"], -1)
    later = tuple(shifted(v, -1) for v in future)
    return outer_dot(jnp.concatenate(later, axis=1).astype(bf16), tables["read_back"])


def long_moments(rows, grads, tables, before, chunk):
    added = halves(row_dot(rows, tables["ages_slope"]))
    late = cmul(tables["decay"], before)
    added = tuple(a + chunk * b for a, b in zip(added, late))
    slope_before = tuple(shifted(v, 1) for v in chunk_scan(added, tables["decay"], 1))
    read = halves(row_dot(grads, tables["leads"]))
    slope = halves(row_dot(grads, tables["leads_slope"]))
    total = lambda pair: tuple(jnp.sum(v, axis=0, keepdims=True) for v in pair)
    moment = total(cmul(read, before))
    first = cmul(slope, before)
    second = cmul(read, slope_before)
    return moment, total((first[0] + second[0], first[1] + second[1]))


def lag_values(log_rate, freq, coef, lags):
    states = log_rate.shape[1]
    rate = jnp.exp(log_rate)
    scale = jnp.sqrt(2.0 * rate)
    steps = jnp.arange(lags).astype(f32)
    real, imaginary = powers(rate[:, :, None], freq[:, :, None], steps)
    weights = (scale * coef[:, :states], scale * coef[:, states:])
    taps = jnp.sum(weights[0][:, :, None] * real - weights[1][:, :, None] * imaginary, axis=1)
    return taps, (real, imaginary)


def local(*args):
    Folding.last = None
    return layer(*args)


def layer(
    feats_long,
    feats_short,
    long_length,
    short_groups,
    freq_start,
    freq_width,
    time_start,
    time_width,
    stem_weight,
    norm_gains,
    ffn1_up,
    ffn1_down,
    mixer_in,
    mixer_out,
    mixer_log_rate,
    mixer_freq,
    mixer_coef,
    conv_taps,
    ffn2_up,
    ffn2_down,
    cotangent_long,
    cotangent_short,
):
    devices = lax.axis_size("tm") * lax.axis_size("head")
    own = stem_weight.shape[0]
    features = own * devices
    hidden_width = ffn1_up.shape[1]
    mel_bins = feats_long.shape[1]
    stem_width = stem_weight.shape[1]
    gain_count, tap_count = norm_gains.shape[1], conv_taps.shape[1]
    down_rows = ffn1_down.shape[0]
    up_blocks = hidden_width // features
    long_rows = feats_long.shape[0] // 4
    short_rows = feats_short.shape[0] // 4
    lead = long_rows // GROUP
    padded_to = lambda w, lanes: jnp.pad(w, ((0, 0), (0, lanes - w.shape[1])))

    block = stack_rows(
        [ffn1_up, mixer_in[:, :features], ffn1_down, stem_weight], features
    )
    split = own * (up_blocks + 1)
    got = [block] + [send_along_z(block, hops) for hops in range(1, grid_of()[0])]
    held = [
        stacked_along_z([g[:split] for g in got]),
        stacked_along_z([g[split:] for g in got]),
    ]
    back = stack_rows([ffn2_up, ffn2_down, mixer_out, mixer_in[:, features:]], features)

    held, mixer_params_own = tied(held, (mixer_log_rate, mixer_freq, mixer_coef))
    log_rate, freq_values, coef_values = (p.astype(f32) for p in mixer_params_own)
    own_taps, lag_powers = lag_values(log_rate, freq_values, coef_values, LAGS)
    shared = jnp.concatenate([own_taps.astype(bf16), norm_gains, conv_taps], axis=1)
    shared = padded_to(shared, -(-shared.shape[1] // 128) * 128)
    shared = exchange(jnp.broadcast_to(shared, (devices,) + shared.shape))

    dims = [[], []]
    orders = [bit_order("x"), bit_order("y")]
    tables_in = (log_rate, freq_values, coef_values)
    for step in range(len(orders[0])):
        for color in range(2):
            name = orders[color][step]
            other = swap(held[color], name)
            dims[color] = [n for n in places() if n in dims[color] or n == name]
            held[color] = joined_at(
                1 + dims[color].index(name), held[color], other, my_bit(name)
            )
        if step == 0:
            held, (tables_in, back) = tied(held, (tables_in, back))
    back_full = lax.all_gather(back, AXES, axis=0)
    tables = long_tables(*tables_in, long_rows)
    core = ("head", 0)
    other = [swap(h, core) for h in held]

    def assembled(color, begin, count, lanes=features):
        part = lambda v: v[..., begin : begin + count, :lanes]
        full = joined_at(1 + len(dims[color]), part(held[color]), part(other[color]), my_bit(core))
        return full.reshape(-1, lanes)

    up_first = [assembled(0, i * own, own) for i in range(up_blocks)]
    proj_inner = assembled(0, up_blocks * own, own)
    down_first = assembled(1, 0, down_rows)
    stem_full = assembled(1, down_rows, own)

    shared = shared.reshape(features, -1).astype(f32).T
    lag_taps = shared[:LAGS]
    lag_flipped = lag_taps[::-1]
    gains = shared[LAGS : LAGS + gain_count]
    taps = padded_to(shared[LAGS + gain_count : LAGS + gain_count + tap_count].T, 16).T

    mel_index = jnp.arange(mel_bins)
    mel_band = (mel_index >= freq_start[0]) & (mel_index < freq_start[0] + freq_width[0])
    freq_keep = (1 - mel_band.astype(jnp.int32)).astype(bf16)
    row_index = jnp.arange(4 * short_rows)
    time_blank = (row_index >= time_start[0]) & (row_index < time_start[0] + time_width[0])
    time_keep = (1 - time_blank.astype(jnp.int32)).astype(bf16)
    stacked = jnp.concatenate(
        [
            (feats_long * freq_keep[None, :]).reshape(long_rows, 4 * mel_bins),
            (feats_short * freq_keep[None, :] * time_keep[:, None]).reshape(
                short_rows, 4 * mel_bins
            ),
        ],
        axis=0,
    )
    stacked = padded_to(stacked, features)
    position = lax.axis_index(AXES) * long_rows + jnp.arange(long_rows)
    valid_long = (position < long_length[0]).astype(f32)
    valid = jnp.concatenate([valid_long, jnp.ones((short_rows,), f32)])[:, None]
    valid_b = valid.astype(bf16)

    residual = outer_dot(stacked, stem_full)
    ffn_first, kept_first = ffn_forward(residual, gains[0], up_first, down_first)
    residual1 = residual + 0.5 * ffn_first
    hat2, scale2 = norm(residual1)
    normed2 = (hat2 * gains[1]).astype(bf16)
    inputs_b = row_dot(normed2, proj_inner).astype(bf16)
    source_b = inputs_b * valid_b

    def to_owner(rows):
        return rows.T.reshape(devices, 8, own * long_rows // 8)

    def at_owner(rows):
        return exchange(rows).reshape(devices, own * long_rows)

    def from_owner(rows):
        return exchange(rows.astype(bf16).reshape(devices, 8, own * long_rows // 8))

    def at_home(rows):
        return rows.reshape(features, long_rows).T.astype(f32)

    long_in, normed2 = tied(to_owner(source_b[:long_rows]), normed2)
    long_in = at_owner(long_in)
    carried, before = long_forward(long_in, tables)
    carried, source_b = tied(carried.astype(bf16), source_b)
    carried = from_owner(carried)
    mixed = mix_forward(lead, short_groups, source_b, lag_taps)
    up_second = [
        back_full[:, i : i + own].reshape(features, features)
        for i in range(0, own * up_blocks, own)
    ]
    place = own * up_blocks
    down_second = back_full[:, place : place + down_rows].reshape(hidden_width, features)
    place += down_rows
    proj_out = back_full[:, place : place + own].reshape(features, features)
    proj_gate = back_full[:, place + own :].reshape(features, features)
    gates = row_dot(normed2, proj_gate)
    gate_act = jax.nn.silu(gates)

    below = lambda v: jnp.pad(v, ((0, short_rows), (0, 0)))
    mixed = (mixed + below(at_home(carried))).astype(bf16).astype(f32)
    inputs_f = inputs_b.astype(f32)
    joined = mixed + gains[5] * inputs_f
    gated_b = (joined * gate_act).astype(bf16)

    residual2 = residual1 + row_dot(gated_b, proj_out)
    hat3, scale3 = norm(residual2)
    spread_b = (hat3 * gains[2]).astype(bf16) * valid_b
    rim = edges(spread_b[:long_rows], TILE)
    pre = conv_forward(lead, tap_count, short_groups, spread_b, rim, taps)
    residual3 = residual2 + jax.nn.silu(pre)
    ffn_second, kept_second = ffn_forward(residual3, gains[3], up_second, down_second)
    residual4 = residual3 + 0.5 * ffn_second
    hat5, scale5 = norm(residual4)
    final = (hat5 * gains[4]).astype(bf16)

    cotangent = jnp.concatenate([cotangent_long, cotangent_short], axis=0).astype(f32)
    grad4, grad_gain4 = norm_back(cotangent, gains[4], hat5, scale5)
    grad_b = (0.5 * grad4).astype(bf16)
    grad_hidden = hidden_grad(grad_b, kept_second, down_second)
    normed, _, active, hat, scale = kept_second
    by_owner = lambda g: g.astype(bf16).reshape(devices, -1, g.shape[1])
    piece, grad_gain3 = norm_back(back_through(grad_hidden, up_second), gains[3], hat, scale)
    grad3 = grad4 + piece
    grad_pre_b = (grad3 * silu_slope(pre)).astype(bf16)
    grad_pre_b, (normed, active) = tied(grad_pre_b, (normed, active))
    grad_rim = edges(grad_pre_b[:long_rows], TILE)
    second = Folding(
        [by_owner(inner_dot(normed, grad_hidden)), by_owner(inner_dot(active, grad_b))]
    )
    grad_pre_b = advance([second], grad_pre_b)
    grad_spread, small_rows = conv_backward(
        lead, tap_count, short_groups, grad_pre_b, grad_rim, spread_b, rim, taps
    )
    piece, grad_gain2 = norm_back(grad_spread * valid, gains[2], hat3, scale3)
    grad2 = grad3 + piece
    grad_out_b = advance([second], grad2.astype(bf16))
    grad_gated = outer_dot(grad_out_b, proj_out)
    grad_joined = grad_gated * gate_act
    grad_mixed_b = grad_joined.astype(bf16)
    grad_in, (grad_mixed_b, gated_b) = tied(
        to_owner(grad_mixed_b[:long_rows]), (grad_mixed_b, gated_b)
    )
    grad_in = at_owner(grad_in)
    grad_gates = grad_gated * joined * silu_slope(gates)
    grad_gain5 = jnp.sum(grad_joined * inputs_f, axis=0)
    grad_proj_out = by_owner(inner_dot(gated_b, grad_out_b))
    half = features // 2
    run = lambda grad, begin, into=None: mix_backward(
        lead, short_groups, grad, source_b, lag_flipped, begin, half, into
    )
    first_half = run(grad_mixed_b, 0)
    later = long_backward(grad_in, tables)
    later, grad_mixed_b = tied(later.astype(bf16), grad_mixed_b)
    later = from_owner(later)
    grad_mixed_b = advance([second], grad_mixed_b)
    grad_source, grad_lags = run(grad_mixed_b, 1, first_half)
    grad_source = (grad_source + below(at_home(later))).astype(bf16).astype(f32)
    grad_inner_b = (grad_source * valid + gains[5] * grad_joined).astype(bf16)
    grad_inner_b = advance([second], grad_inner_b)
    grad_gates_b = grad_gates.astype(bf16)
    back = outer_dot(grad_inner_b, proj_inner) + outer_dot(grad_gates_b, proj_gate)
    piece, grad_gain1 = norm_back(back, gains[1], hat2, scale2)
    grad1 = grad2 + piece
    grad_b = (0.5 * grad1).astype(bf16)
    normed, _, active, hat, scale = kept_first
    unit = (jnp.arange(LAGS)[:, None] == jnp.arange(features)[None, :]).astype(bf16)
    early_out = jnp.concatenate(
        [
            by_owner(inner_dot(normed2, grad_inner_b)),
            by_owner(inner_dot(normed2, grad_gates_b)),
            grad_proj_out,
            by_owner(inner_dot(grad_lags.astype(bf16), unit)),
        ],
        axis=1,
    )
    early = Folding([by_owner(inner_dot(active, grad_b)), early_out], 0)
    grad_b = advance([early], grad_b)
    grad_hidden = hidden_grad(grad_b, kept_first, down_first)
    grad_hidden = advance([second], grad_hidden)
    late = Folding([by_owner(inner_dot(normed, grad_hidden))], 0)
    grad_hidden = advance([late, early], grad_hidden)
    piece, grad_gain0 = norm_back(back_through(grad_hidden, up_first), gains[0], hat, scale)
    grad_zero_b = settle(second, advance([late], (grad1 + piece).astype(bf16)))

    row = jnp.arange(SMALL_ROWS)[:, None]
    gain_rows = [grad_gain0, grad_gain1, grad_gain2, grad_gain3, grad_gain4, grad_gain5]
    for k, grad_gain in enumerate(gain_rows):
        small_rows = jnp.where(row == k, grad_gain[None, :], small_rows)
    lane = jnp.arange(features)[None, :] - stem_width
    place = jnp.where(lane < gain_count, lane, lane - gain_count + TILE)
    small_unit = ((place == row) & (lane >= 0) & (lane < gain_count + tap_count)).astype(bf16)
    small = inner_dot(grad_zero_b, stacked) + inner_dot(small_rows.astype(bf16), small_unit)
    small = exchange(by_owner(small))
    grad_zero_b = advance([early], grad_zero_b)
    grad_stacked = row_dot(grad_zero_b, stem_full)[:, :stem_width]
    freq_float = freq_keep.astype(f32)
    time_float = time_keep.astype(f32)
    input_long = (
        grad_stacked[:long_rows].reshape(4 * long_rows, mel_bins) * freq_float[None, :]
    ).astype(bf16)
    input_short = (
        grad_stacked[long_rows:].reshape(4 * short_rows, mel_bins)
        * freq_float[None, :]
        * time_float[:, None]
    ).astype(bf16)
    moment_in, input_long, input_short = advance(
        [early, late], ((long_in, grad_in, before), input_long, input_short)
    )
    for fold in (second, early):
        while not fold.done:
            advance([fold])
    moment_in = settle(second, moment_in)
    moment, moment_slope = long_moments(*moment_in[:2], tables, moment_in[2], long_rows)
    sum_up2, sum_down2 = second.result()
    sum_early = early.result()
    grad_small = jnp.sum(small.astype(f32), axis=0)
    (sum_up1,) = late.result()
    sum_down1, rest = sum_early
    sum_in = jnp.concatenate([rest[:own], rest[own : 2 * own]], axis=1)
    sum_out = rest[2 * own : 3 * own]
    lag_grad = rest[3 * own :, :LAGS]

    states = log_rate.shape[1]
    steps = jnp.arange(LAGS).astype(f32)
    near = tuple(jnp.sum(lag_grad[:, None, :] * p, axis=2) for p in lag_powers)
    near_slope = tuple(jnp.sum((lag_grad * steps)[:, None, :] * p, axis=2) for p in lag_powers)
    shape = (own, states)
    moment = tuple(a.reshape(shape) + b for a, b in zip(moment, near))
    moment_slope = tuple(a.reshape(shape) + b for a, b in zip(moment_slope, near_slope))
    weight = tuple(w.reshape(shape) for w in tables["weight"])
    rate = tables["rate"].reshape(shape)
    scale = tables["scale"].reshape(shape)
    pulled = cmul(weight, moment)
    pulled_slope = cmul(weight, moment_slope)
    grad_rate = 0.5 * pulled[0] - rate * pulled_slope[0]
    grad_freq = -pulled_slope[1]
    grad_coef = jnp.concatenate([scale * moment[0], -scale * moment[1]], axis=1)

    return (
        final[:long_rows],
        final[long_rows:],
        input_long,
        input_short,
        grad_small[:, :stem_width],
        grad_small[:, stem_width : stem_width + gain_count],
        sum_up1,
        sum_down1,
        sum_in,
        sum_out,
        grad_rate,
        grad_freq,
        grad_coef,
        grad_small[:, stem_width + gain_count : stem_width + gain_count + tap_count],
        sum_up2,
        sum_down2,
    )


def solution(mesh):
    rows = P(AXES, None)
    flat = P(AXES)
    return jax.shard_map(
        local,
        mesh=mesh,
        in_specs=(rows, rows, P(), rows, flat, flat, flat, flat) + (rows,) * 14,
        out_specs=(rows,) * 16,
        check_vma=False,
    )
```

```python
from functools import partial

import jax
import jax.numpy as jnp
from jax import lax
from jax.experimental import pallas as pl
from jax.experimental.pallas import tpu as pltpu
from jax.sharding import PartitionSpec as P

GROUP = 32
LAGS = 192
TILE = 8
LANES = 256
SMALL_ROWS = 32
AXES = ("tm", "head")

f32 = jnp.float32
bf16 = jnp.bfloat16


def bits_of(axis):
    return (lax.axis_size(axis) - 1).bit_length()


def grid_of():
    tm, head = lax.axis_size("tm"), lax.axis_size("head")
    y = 1 << ((bits_of("tm") - 1) // 2)
    return tm // y, y, head // 2, 2


def places():
    _, y, x, _ = grid_of()
    names = [("tm", b) for b in reversed(range(y.bit_length() - 1))]
    return names + [("head", b) for b in reversed(range(bits_of("head")))]


def bit_order(first):
    heads = [n for n in places() if n[0] == "head" and n[1] > 0]
    tms = [n for n in places() if n[0] == "tm"]
    return heads + tms if first == "x" else tms + heads


def my_bit(name):
    return (lax.axis_index(name[0]) >> name[1]) & 1


def swap(value, name):
    axis, bit = name
    return lax.ppermute(value, axis, [(i, i ^ (1 << bit)) for i in range(lax.axis_size(axis))])


def send_along_z(value, hops):
    z, y, _, _ = grid_of()
    pairs = [(i, (i // y + hops) % z * y + i % y) for i in range(z * y)]
    return lax.ppermute(value, "tm", pairs)


def my_z():
    return lax.axis_index("tm") // grid_of()[1]


def joined_at(dim, mine, other, place):
    shape = mine.shape[:dim] + (2,) + mine.shape[dim:]
    index = lax.broadcasted_iota(jnp.int32, shape, dim)
    wide = lambda v: jnp.broadcast_to(jnp.expand_dims(v, dim), shape)
    return jnp.where(index == place, wide(mine), wide(other))


def tied(first, then):
    return lax.optimization_barrier((first, then))


def stacked_along_z(got):
    z = len(got)
    index = lax.broadcasted_iota(jnp.int32, (z,) + got[0].shape, 0)
    held = jnp.broadcast_to(got[0], index.shape)
    for hops in range(1, z):
        held = jnp.where(index == (my_z() - hops) % z, got[hops], held)
    return held


def pick(array, index):
    starts = [jnp.int32(0) if i is None else i for i in index]
    sizes = [n if i is None else 1 for n, i in zip(array.shape, index)]
    kept = [n for n, i in zip(array.shape, index) if i is None]
    tail = list(array.shape[len(index) :])
    starts += [jnp.int32(0)] * len(tail)
    return lax.dynamic_slice(array, starts, sizes + tail).reshape(kept + tail).astype(f32)


def settle(fold, values):
    newest, values = tied([terms[-1][0] for terms in fold.terms], values)
    for terms, array in zip(fold.terms, newest):
        terms[-1] = (array, terms[-1][1])
    return values


def all_bits():
    bits = [("tm", b) for b in reversed(range(bits_of("tm")))]
    return bits + [("head", b) for b in reversed(range(bits_of("head")))]


class Folding:
    last = None

    def __init__(self, grads, join=None):
        names = all_bits()
        self.high = [n for n in names if n[0] == "tm" and n not in places()]
        self.terms = [[(g.reshape((2,) * len(names) + g.shape[1:]), names)] for g in grads]
        firsts = "y" if len(grads) == 1 else "xy"
        self.todo = [[("head", 0)] + bit_order(first) for first in firsts]
        if join is None:
            self.todo = [todo + self.high[::-1] for todo in self.todo]
        self.fixed = [{} for _ in grads]
        self.join = join
        self.done = False

    def total(self, color, fixed):
        value = None
        for array, names in self.terms[color]:
            piece = pick(array, [fixed.get(name) for name in names])
            value = piece if value is None else value + piece
        return value

    def at_z(self, color, z):
        bits = {name: (z >> place) & 1 for place, name in enumerate(self.high[::-1])}
        return self.total(color, {**self.fixed[color], **bits})

    def load(self):
        if Folding.last is not None:
            newest = [terms[-1][0] for terms in self.terms]
            newest = tied(Folding.last, newest)[1]
            for terms, array in zip(self.terms, newest):
                terms[-1] = (array, terms[-1][1])
        colors = range(len(self.terms))
        values = []
        if self.todo[0]:
            for color in colors:
                name = self.todo[color][0]
                fixed = {**self.fixed[color], name: 1 - my_bit(name)}
                values.append(self.total(color, fixed).astype(bf16))
        elif self.join is not None:
            z = grid_of()[0]
            for hops in range(1, z):
                parts = [self.at_z(c, (my_z() + hops) % z).astype(bf16) for c in colors]
                values.append(jnp.concatenate(parts, axis=self.join))
        Folding.last = values or None
        return values

    def send(self, values):
        if self.todo[0]:
            for color, value in enumerate(values):
                name = self.todo[color].pop(0)
                got = swap(value, name)
                self.fixed[color][name] = my_bit(name)
                left = [n for n in all_bits() if n not in self.fixed[color]]
                self.terms[color].append((got, left))
        else:
            self.got = [send_along_z(v, hops + 1).astype(f32) for hops, v in enumerate(values)]
            self.done = True
        if self.join is None:
            self.done = not self.todo[0]

    def result(self):
        while not self.done:
            advance([self])
        if self.join is None:
            return [self.total(c, self.fixed[c]) for c in range(len(self.terms))]
        sums = [self.at_z(c, my_z()) for c in range(len(self.terms))]
        if len(sums) == 1:
            return [sums[0] + sum(self.got)]
        cut = sums[0].shape[self.join]
        for got in self.got:
            pieces = (got[:cut], got[cut:]) if self.join == 0 else (got[:, :cut], got[:, cut:])
            sums = [a + b for a, b in zip(sums, pieces)]
        return sums


def advance(folds, values=()):
    for fold in folds:
        if not fold.done:
            load, values = tied(fold.load(), values)
            fold.send(load)
    return values


def exchange(rows):
    return lax.all_to_all(rows, AXES, split_axis=0, concat_axis=0, tiled=True)


def edges(x, width):
    size = lax.axis_size("tm") * lax.axis_size("head")
    up = [(i, i + 1) for i in range(size - 1)]
    down = [(j, i) for i, j in up]
    before = lax.ppermute(x[x.shape[0] - width :], AXES, up)
    after = lax.ppermute(x[:width], AXES, down)
    return before, after


def row_dot(a, b):
    return jnp.dot(a, b, preferred_element_type=f32)


def inner_dot(a, b):
    return lax.dot_general(a, b, (((0,), (0,)), ((), ())), preferred_element_type=f32)


def outer_dot(a, b):
    return lax.dot_general(a, b, (((1,), (1,)), ((), ())), preferred_element_type=f32)


def norm(values):
    centred = values - jnp.mean(values, axis=-1, keepdims=True)
    scale = lax.rsqrt(jnp.mean(centred * centred, axis=-1, keepdims=True) + 1e-05)
    return centred * scale, scale


def norm_back(grad, gain, hat, scale):
    e = grad * gain
    back = e - jnp.mean(e, axis=-1, keepdims=True)
    back = (back - hat * jnp.mean(e * hat, axis=-1, keepdims=True)) * scale
    return back, jnp.sum(grad * hat, axis=0)


def silu_slope(values):
    logistic = jax.nn.sigmoid(values)
    return logistic * (1.0 + values * (1.0 - logistic))


def ffn_forward(residual, gain, up, down):
    hat, scale = norm(residual)
    normed = (hat * gain).astype(bf16)
    hidden = jnp.concatenate([row_dot(normed, part) for part in up], axis=1)
    active = jax.nn.silu(hidden).astype(bf16)
    return row_dot(active, down), (normed, hidden, active, hat, scale)


def column_blocks(x, width):
    return [x[:, i : i + width] for i in range(0, x.shape[1], width)]


def back_through(grad, parts):
    blocks = column_blocks(grad, grad.shape[1] // len(parts))
    return sum(outer_dot(block, part) for block, part in zip(blocks, parts))


def hidden_grad(grad_b, kept, down):
    return (outer_dot(grad_b, down) * silu_slope(kept[1])).astype(bf16)


def utterance_edges(groups, lead, blocks, block):
    first = jnp.int32(0)
    after = jnp.int32(lead)
    begin = jnp.int32(lead)
    for u in range(groups.shape[1]):
        end = begin + groups[0, u]
        inside = block >= begin
        first = jnp.where(inside, begin, first)
        after = jnp.where(inside, end, after)
        begin = end
    return first, after


def lag_tile(table, shift, tile):
    if isinstance(tile, int):
        return table[shift, tile * TILE : (tile + 1) * TILE, :]
    return table[shift, pl.ds(pl.multiple_of(tile * TILE, TILE), TILE), :]


def mix_forward_kernel(lead, groups, source, taps, out, rows_f, padded, table):
    blocks = source.shape[0] // GROUP
    tiles = GROUP // TILE
    rows_f[...] = source[...].astype(f32)
    padded[0:TILE, :] = jnp.zeros((TILE, padded.shape[1]), f32)
    padded[TILE:, :] = taps[...]
    for q in range(TILE):
        table[q] = padded[TILE - q : TILE - q + LAGS, :]

    def tile_of(ref, block, i):
        return ref[pl.ds(pl.multiple_of(block * GROUP + i * TILE, TILE), TILE), :]

    def one(block, carry):
        first, _ = utterance_edges(groups, lead, blocks, block)
        sums = [jnp.zeros((TILE, rows_f.shape[1]), f32) for _ in range(tiles)]
        own = [tile_of(rows_f, block, j) for j in range(tiles)]
        for q in range(TILE):
            lags = [lag_tile(table, q, d) for d in range(tiles)]
            for j in range(tiles):
                row = own[j][q : q + 1, :]
                for i in range(j, tiles):
                    sums[i] = sums[i] + lags[i - j] * row

        def pair(other, sums):
            sums = list(sums)
            base = (block - other) * tiles
            own = [tile_of(rows_f, other, j) for j in range(tiles)]
            for q in range(TILE):
                lags = {d: lag_tile(table, q, base + d) for d in range(1 - tiles, tiles)}
                for j in range(tiles):
                    row = own[j][q : q + 1, :]
                    for i in range(tiles):
                        sums[i] = sums[i] + lags[i - j] * row
            return tuple(sums)

        sums = lax.fori_loop(first, block, pair, tuple(sums))
        for i in range(tiles):
            out[pl.ds(pl.multiple_of(block * GROUP + i * TILE, TILE), TILE), :] = sums[i]
        return carry

    lax.fori_loop(0, blocks, one, 0)


def mix_backward_kernel(
    lead, groups, grad, source, taps_flipped, out, grad_taps, grad_f, rows_f, padded, table, sums_q
):
    blocks = source.shape[0] // GROUP
    tiles = GROUP // TILE
    top = LAGS // TILE - 1
    grad_f[...] = grad[...].astype(f32)
    rows_f[...] = source[...].astype(f32)
    padded[0:LAGS, :] = taps_flipped[...]
    padded[LAGS:, :] = jnp.zeros((TILE, padded.shape[1]), f32)
    for q in range(TILE):
        table[q] = padded[q : q + LAGS, :]
        sums_q[q] = jnp.zeros(sums_q.shape[1:], f32)

    def tile_of(ref, block, i):
        return ref[pl.ds(pl.multiple_of(block * GROUP + i * TILE, TILE), TILE), :]

    def add_to(q, tile, value):
        if isinstance(tile, int):
            place = slice(tile * TILE, (tile + 1) * TILE)
        else:
            place = pl.ds(pl.multiple_of(tile * TILE, TILE), TILE)
        sums_q[q, place, :] = sums_q[q, place, :] + value

    def one(block, carry):
        _, after = utterance_edges(groups, lead, blocks, block)
        sums = [jnp.zeros((TILE, rows_f.shape[1]), f32) for _ in range(tiles)]
        own = [tile_of(rows_f, block, j) for j in range(tiles)]
        here = [tile_of(grad_f, block, i) for i in range(tiles)]
        for q in range(TILE):
            lags = [lag_tile(table, TILE - 1 - q, top - d) for d in range(tiles)]
            for i in range(tiles):
                row = here[i][q : q + 1, :]
                for j in range(i + 1):
                    sums[j] = sums[j] + lags[i - j] * row
            rows = [own[j][q : q + 1, :] for j in range(tiles)]
            for d in range(tiles):
                total = here[d] * rows[0]
                for j in range(1, tiles - d):
                    total = total + here[d + j] * rows[j]
                add_to(q, d, total)

        def pair(other, sums):
            sums = list(sums)
            base = (other - block) * tiles
            here = [tile_of(grad_f, other, i) for i in range(tiles)]
            for q in range(TILE):
                lags = {
                    d: lag_tile(table, TILE - 1 - q, top - base - d)
                    for d in range(1 - tiles, tiles)
                }
                for i in range(tiles):
                    row = here[i][q : q + 1, :]
                    for j in range(tiles):
                        sums[j] = sums[j] + lags[i - j] * row
                rows = [own[j][q : q + 1, :] for j in range(tiles)]
                for d in range(1 - tiles, tiles):
                    total = None
                    for j in range(tiles):
                        if 0 <= j + d < tiles:
                            term = here[j + d] * rows[j]
                            total = term if total is None else total + term
                    add_to(q, base + d, total)
            return tuple(sums)

        sums = lax.fori_loop(block + 1, after, pair, tuple(sums))
        for j in range(tiles):
            out[pl.ds(pl.multiple_of(block * GROUP + j * TILE, TILE), TILE), :] = sums[j]
        return carry

    lax.fori_loop(0, blocks, one, 0)
    total = sums_q[0, 0:LAGS, :]
    for q in range(1, TILE):
        total = total + sums_q[q, q : q + LAGS, :]
    grad_taps[...] = total


def mixer_params():
    return pltpu.CompilerParams(vmem_limit_bytes=40 * 1024 * 1024)


def mix_forward(lead, groups, source, taps):
    rows, features = source.shape
    lanes = min(LANES, features)
    column = lambda count: pl.BlockSpec((count, lanes), lambda i: (0, i))
    return pl.pallas_call(
        partial(mix_forward_kernel, lead),
        out_shape=jax.ShapeDtypeStruct((rows, features), f32),
        grid=(features // lanes,),
        in_specs=[pl.BlockSpec(memory_space=pltpu.SMEM), column(rows), column(LAGS)],
        out_specs=column(rows),
        scratch_shapes=[
            pltpu.VMEM((rows, lanes), f32),
            pltpu.VMEM((LAGS + TILE, lanes), f32),
            pltpu.VMEM((TILE, LAGS, lanes), f32),
        ],
        compiler_params=mixer_params(),
        cost_estimate=pl.CostEstimate(
            flops=30000 * rows * features, bytes_accessed=rows * features * 8, transcendentals=0
        ),
        name="mix_forward",
    )(groups, source, taps)


def mix_backward(lead, groups, grad, source, taps_flipped, begin, width, into=None):
    rows, features = source.shape
    column = lambda count: pl.BlockSpec((count, width), lambda i: (0, begin))
    kept = [] if into is None else list(into)
    kernel = partial(mix_backward_kernel, lead)

    def body(*refs):
        kernel(*refs[:4], *refs[4 + len(kept) :])

    return pl.pallas_call(
        body,
        out_shape=(
            jax.ShapeDtypeStruct((rows, features), f32),
            jax.ShapeDtypeStruct((LAGS, features), f32),
        ),
        grid=(1,),
        in_specs=[
            pl.BlockSpec(memory_space=pltpu.SMEM),
            column(rows),
            column(rows),
            column(LAGS),
        ]
        + [pl.BlockSpec(memory_space=pl.ANY)] * len(kept),
        out_specs=(column(rows), column(LAGS)),
        scratch_shapes=[
            pltpu.VMEM((rows, width), f32),
            pltpu.VMEM((rows, width), f32),
            pltpu.VMEM((LAGS + TILE, width), f32),
            pltpu.VMEM((TILE, LAGS, width), f32),
            pltpu.VMEM((TILE, LAGS + TILE, width), f32),
        ],
        input_output_aliases={4 + i: i for i in range(len(kept))},
        compiler_params=mixer_params(),
        cost_estimate=pl.CostEstimate(
            flops=10000 * rows * width, bytes_accessed=rows * width * 8, transcendentals=0
        ),
        name="mix_backward",
    )(groups, grad, source, taps_flipped, *kept)


def fill_window(window, rows, before, after, lead, groups, block, blocks):
    first, stop = utterance_edges(groups, lead, blocks, block)
    place = lambda start, count: pl.ds(pl.multiple_of(start, 2 * TILE), count)
    window[TILE : TILE + GROUP, :] = rows[place(block * GROUP, GROUP), :].astype(f32)
    empty = jnp.zeros((TILE, window.shape[1]), f32)
    start = jnp.maximum(block * GROUP - 2 * TILE, 0)
    left = rows[place(start, 2 * TILE), :].astype(f32)[TILE:]
    left = jnp.where(block == 0, before[...].astype(f32), left)
    window[0:TILE, :] = jnp.where((block == 0) | (block > first), left, empty)
    start = jnp.minimum((block + 1) * GROUP, (blocks - 1) * GROUP)
    right = rows[place(start, 2 * TILE), :].astype(f32)[:TILE]
    right = jnp.where(block == lead - 1, after[...].astype(f32), right)
    keep = (block == lead - 1) | (block + 1 < stop)
    window[TILE + GROUP :, :] = jnp.where(keep, right, empty)


def conv_forward_kernel(lead, count, groups, rows, before, after, taps, out, window):
    blocks = rows.shape[0] // GROUP
    shift = TILE - count // 2

    def one(block, carry):
        fill_window(window, rows, before, after, lead, groups, block, blocks)
        total = None
        for k in range(count):
            term = window[shift + k : shift + k + GROUP, :] * taps[k : k + 1, :]
            total = term if total is None else total + term
        out[pl.ds(pl.multiple_of(block * GROUP, GROUP), GROUP), :] = total
        return carry

    lax.fori_loop(0, blocks, one, 0)


def conv_backward_kernel(
    lead, count, groups, grads, g_before, g_after, rows, before, after, taps, out, grad_taps,
    g_window, window, sums,
):
    blocks = rows.shape[0] // GROUP
    shift = TILE - count // 2
    sums[...] = jnp.zeros(sums.shape, f32)

    def one(block, carry):
        fill_window(g_window, grads, g_before, g_after, lead, groups, block, blocks)
        fill_window(window, rows, before, after, lead, groups, block, blocks)
        here = g_window[TILE : TILE + GROUP, :]
        total = None
        for k in range(count):
            lag = shift + count - 1 - k
            term = g_window[lag : lag + GROUP, :] * taps[k : k + 1, :]
            total = term if total is None else total + term
            product = here * window[shift + k : shift + k + GROUP, :]
            part = product[0:TILE]
            for i in range(TILE, GROUP, TILE):
                part = part + product[i : i + TILE]
            sums[k] = sums[k] + part
        out[pl.ds(pl.multiple_of(block * GROUP, GROUP), GROUP), :] = total
        return carry

    lax.fori_loop(0, blocks, one, 0)
    below = grad_taps.shape[0] - TILE - count
    grad_taps[...] = jnp.concatenate(
        [jnp.zeros((TILE, grad_taps.shape[1]), f32)]
        + [jnp.sum(sums[k], axis=0, keepdims=True) for k in range(count)]
        + [jnp.zeros((below, grad_taps.shape[1]), f32)],
        axis=0,
    )


def conv_call(kernel, lead, groups, arrays, outs, scratch, name):
    lanes = min(LANES, arrays[0].shape[1])
    column = lambda count: pl.BlockSpec((count, lanes), lambda i: (0, i))
    rows, features = arrays[0].shape
    return pl.pallas_call(
        kernel,
        out_shape=tuple(jax.ShapeDtypeStruct((n, features), f32) for n in outs),
        grid=(features // lanes,),
        in_specs=[pl.BlockSpec(memory_space=pltpu.SMEM)] + [column(a.shape[0]) for a in arrays],
        out_specs=tuple(column(n) for n in outs),
        scratch_shapes=[pltpu.VMEM(shape + (lanes,), f32) for shape in scratch],
        compiler_params=mixer_params(),
        cost_estimate=pl.CostEstimate(
            flops=4000 * rows * features, bytes_accessed=rows * features * 8, transcendentals=0
        ),
        name=name,
    )(groups, *arrays)


def conv_forward(lead, count, groups, rows, rim, taps):
    return conv_call(
        partial(conv_forward_kernel, lead, count),
        lead,
        groups,
        [rows, *rim, taps],
        [rows.shape[0]],
        [(GROUP + 2 * TILE,)],
        "conv_forward",
    )[0]


def conv_backward(lead, count, groups, grads, g_rim, rows, rim, taps):
    return conv_call(
        partial(conv_backward_kernel, lead, count),
        lead,
        groups,
        [grads, *g_rim, rows, *rim, taps],
        [rows.shape[0], SMALL_ROWS],
        [(GROUP + 2 * TILE,), (GROUP + 2 * TILE,), (count, TILE)],
        "conv_backward",
    )


def stack_rows(pieces, lanes):
    pieces = list(pieces)
    if any(p.shape[0] % 16 for p in pieces):
        fill = lambda p: jnp.pad(p, ((0, 0), (0, lanes - p.shape[1])))
        blocks = [b for p in pieces for b in (column_blocks(p, lanes) if p.shape[1] > lanes else [p])]
        return jnp.concatenate([fill(b) for b in blocks], axis=0)
    total = sum(p.shape[0] * -(-p.shape[1] // lanes) for p in pieces)

    def kernel(*refs):
        out, row = refs[-1], 0
        for ref in refs[:-1]:
            count, width = ref.shape
            for begin in range(0, width, lanes):
                here = min(lanes, width - begin)
                if here < lanes:
                    out[row : row + count, :] = jnp.zeros((count, lanes), out.dtype)
                out[row : row + count, 0:here] = ref[:, begin : begin + here]
                row += count

    return pl.pallas_call(
        kernel,
        out_shape=jax.ShapeDtypeStruct((total, lanes), pieces[0].dtype),
        in_specs=[pl.BlockSpec(memory_space=pltpu.VMEM)] * len(pieces),
        out_specs=pl.BlockSpec(memory_space=pltpu.VMEM),
        compiler_params=mixer_params(),
        name="stack_rows",
    )(*pieces)


def cmul(a, b):
    return (a[0] * b[0] - a[1] * b[1], a[0] * b[1] + a[1] * b[0])


def powers(rate, freq, steps):
    decay = jnp.exp(-rate * steps)
    return decay * jnp.cos(freq * steps), decay * jnp.sin(freq * steps)


def shifted(x, count):
    pad = jnp.zeros((abs(count),) + x.shape[1:], x.dtype)
    if count > 0:
        return jnp.concatenate([pad, x[:-count]], axis=0)
    return jnp.concatenate([x[-count:], pad], axis=0)


def chunk_scan(values, decay, sign):
    count = values[0].shape[0]
    hop = 1
    while hop < count:
        moved = tuple(shifted(v, sign * hop) for v in values)
        added = cmul(decay, moved)
        values = (values[0] + added[0], values[1] + added[1])
        decay = cmul(decay, decay)
        hop *= 2
    return values


def long_tables(log_rate, freq, coef, chunk):
    channels, states = log_rate.shape
    lanes = channels * states
    rate = jnp.exp(log_rate).reshape(1, lanes)
    freq = freq.reshape(1, lanes)
    scale = jnp.sqrt(2.0 * rate)
    weight = (
        scale * coef[:, :states].reshape(1, lanes),
        scale * coef[:, states:].reshape(1, lanes),
    )
    steps = jnp.arange(chunk + 1).astype(f32)[:, None]
    power = powers(rate, freq, steps)
    mask = jnp.arange(channels)[:, None] == (jnp.arange(lanes) // states)[None, :]
    mask = mask.astype(f32)[:, None, :]

    def spread(pair):
        wide = [(mask * part[None]).reshape(channels * chunk, lanes) for part in pair]
        return jnp.concatenate(wide, axis=1).astype(bf16)

    ages = tuple(p[:chunk][::-1] for p in power)
    leads = tuple(p[1:] for p in power)
    weighted = lambda pair: cmul(weight, pair)
    signed = lambda pair: (pair[0], -pair[1])
    return {
        "ages": spread(ages),
        "ages_slope": spread(tuple(a * steps[:chunk][::-1] for a in ages)),
        "leads": spread(leads),
        "leads_slope": spread(tuple(a * steps[1:] for a in leads)),
        "read": spread(signed(weighted(leads))),
        "read_back": spread(signed(weighted(ages))),
        "decay": powers(rate, freq, jnp.float32(chunk)),
        "rate": rate,
        "scale": scale,
        "weight": weight,
    }


def halves(x):
    lanes = x.shape[1] // 2
    return x[:, :lanes], x[:, lanes:]


def long_forward(rows, tables):
    added = halves(row_dot(rows, tables["ages"]))
    state = chunk_scan(added, tables["decay"], 1)
    before = tuple(shifted(v, 1) for v in state)
    carried = outer_dot(jnp.concatenate(before, axis=1).astype(bf16), tables["read"])
    return carried, before


def long_backward(grads, tables):
    read = halves(row_dot(grads, tables["leads"]))
    future = chunk_scan(read, tables["decay"], -1)
    later = tuple(shifted(v, -1) for v in future)
    return outer_dot(jnp.concatenate(later, axis=1).astype(bf16), tables["read_back"])


def long_moments(rows, grads, tables, before, chunk):
    added = halves(row_dot(rows, tables["ages_slope"]))
    late = cmul(tables["decay"], before)
    added = tuple(a + chunk * b for a, b in zip(added, late))
    slope_before = tuple(shifted(v, 1) for v in chunk_scan(added, tables["decay"], 1))
    read = halves(row_dot(grads, tables["leads"]))
    slope = halves(row_dot(grads, tables["leads_slope"]))
    total = lambda pair: tuple(jnp.sum(v, axis=0, keepdims=True) for v in pair)
    moment = total(cmul(read, before))
    first = cmul(slope, before)
    second = cmul(read, slope_before)
    return moment, total((first[0] + second[0], first[1] + second[1]))


def lag_values(log_rate, freq, coef, lags):
    states = log_rate.shape[1]
    rate = jnp.exp(log_rate)
    scale = jnp.sqrt(2.0 * rate)
    steps = jnp.arange(lags).astype(f32)
    real, imaginary = powers(rate[:, :, None], freq[:, :, None], steps)
    weights = (scale * coef[:, :states], scale * coef[:, states:])
    taps = jnp.sum(weights[0][:, :, None] * real - weights[1][:, :, None] * imaginary, axis=1)
    return taps, (real, imaginary)


def local(*args):
    Folding.last = None
    return layer(*args)


def layer(
    feats_long,
    feats_short,
    long_length,
    short_groups,
    freq_start,
    freq_width,
    time_start,
    time_width,
    stem_weight,
    norm_gains,
    ffn1_up,
    ffn1_down,
    mixer_in,
    mixer_out,
    mixer_log_rate,
    mixer_freq,
    mixer_coef,
    conv_taps,
    ffn2_up,
    ffn2_down,
    cotangent_long,
    cotangent_short,
):
    devices = lax.axis_size("tm") * lax.axis_size("head")
    own = stem_weight.shape[0]
    features = own * devices
    hidden_width = ffn1_up.shape[1]
    mel_bins = feats_long.shape[1]
    stem_width = stem_weight.shape[1]
    gain_count, tap_count = norm_gains.shape[1], conv_taps.shape[1]
    down_rows = ffn1_down.shape[0]
    up_blocks = hidden_width // features
    long_rows = feats_long.shape[0] // 4
    short_rows = feats_short.shape[0] // 4
    lead = long_rows // GROUP
    padded_to = lambda w, lanes: jnp.pad(w, ((0, 0), (0, lanes - w.shape[1])))

    block = stack_rows(
        [ffn1_up, mixer_in[:, :features], ffn1_down, stem_weight], features
    )
    split = own * (up_blocks + 1)
    got = [block] + [send_along_z(block, hops) for hops in range(1, grid_of()[0])]
    held = [
        stacked_along_z([g[:split] for g in got]),
        stacked_along_z([g[split:] for g in got]),
    ]
    back = stack_rows([ffn2_up, ffn2_down, mixer_out, mixer_in[:, features:]], features)

    held, mixer_params_own = tied(held, (mixer_log_rate, mixer_freq, mixer_coef))
    log_rate, freq_values, coef_values = (p.astype(f32) for p in mixer_params_own)
    own_taps, lag_powers = lag_values(log_rate, freq_values, coef_values, LAGS)
    shared = jnp.concatenate([own_taps.astype(bf16), norm_gains, conv_taps], axis=1)
    shared = padded_to(shared, -(-shared.shape[1] // 128) * 128)
    shared = exchange(jnp.broadcast_to(shared, (devices,) + shared.shape))

    dims = [[], []]
    orders = [bit_order("x"), bit_order("y")]
    tables_in = (log_rate, freq_values, coef_values)
    for step in range(len(orders[0])):
        for color in range(2):
            name = orders[color][step]
            other = swap(held[color], name)
            dims[color] = [n for n in places() if n in dims[color] or n == name]
            held[color] = joined_at(
                1 + dims[color].index(name), held[color], other, my_bit(name)
            )
        if step == 0:
            held, (tables_in, back) = tied(held, (tables_in, back))
    back_full = lax.all_gather(back, AXES, axis=0)
    tables = long_tables(*tables_in, long_rows)
    shared = shared.reshape(features, -1).astype(f32).T
    held, (tables["ages"], shared) = tied(held, (tables["ages"], shared))
    core = ("head", 0)
    other = [swap(h, core) for h in held]

    def assembled(color, begin, count, lanes=features):
        part = lambda v: v[..., begin : begin + count, :lanes]
        full = joined_at(1 + len(dims[color]), part(held[color]), part(other[color]), my_bit(core))
        return full.reshape(-1, lanes)

    up_first = [assembled(0, i * own, own) for i in range(up_blocks)]
    proj_inner = assembled(0, up_blocks * own, own)
    down_first = assembled(1, 0, down_rows)
    stem_full = assembled(1, down_rows, own)

    lag_taps = shared[:LAGS]
    lag_flipped = lag_taps[::-1]
    gains = shared[LAGS : LAGS + gain_count]
    taps = padded_to(shared[LAGS + gain_count : LAGS + gain_count + tap_count].T, 16).T

    mel_index = jnp.arange(mel_bins)
    mel_band = (mel_index >= freq_start[0]) & (mel_index < freq_start[0] + freq_width[0])
    freq_keep = (1 - mel_band.astype(jnp.int32)).astype(bf16)
    row_index = jnp.arange(4 * short_rows)
    time_blank = (row_index >= time_start[0]) & (row_index < time_start[0] + time_width[0])
    time_keep = (1 - time_blank.astype(jnp.int32)).astype(bf16)
    stacked = jnp.concatenate(
        [
            (feats_long * freq_keep[None, :]).reshape(long_rows, 4 * mel_bins),
            (feats_short * freq_keep[None, :] * time_keep[:, None]).reshape(
                short_rows, 4 * mel_bins
            ),
        ],
        axis=0,
    )
    stacked = padded_to(stacked, features)
    position = lax.axis_index(AXES) * long_rows + jnp.arange(long_rows)
    valid_long = (position < long_length[0]).astype(f32)
    valid = jnp.concatenate([valid_long, jnp.ones((short_rows,), f32)])[:, None]
    valid_b = valid.astype(bf16)

    residual = outer_dot(stacked, stem_full)
    ffn_first, kept_first = ffn_forward(residual, gains[0], up_first, down_first)
    residual1 = residual + 0.5 * ffn_first
    hat2, scale2 = norm(residual1)
    normed2 = (hat2 * gains[1]).astype(bf16)
    inputs_b = row_dot(normed2, proj_inner).astype(bf16)
    source_b = inputs_b * valid_b

    def to_owner(rows):
        return rows.T.reshape(devices, 8, own * long_rows // 8)

    def at_owner(rows):
        return exchange(rows).reshape(devices, own * long_rows)

    def from_owner(rows):
        return exchange(rows.astype(bf16).reshape(devices, 8, own * long_rows // 8))

    def at_home(rows):
        return rows.reshape(features, long_rows).T.astype(f32)

    long_in, normed2 = tied(to_owner(source_b[:long_rows]), normed2)
    long_in = at_owner(long_in)
    carried, before = long_forward(long_in, tables)
    carried, source_b = tied(carried.astype(bf16), source_b)
    carried = from_owner(carried)
    mixed = mix_forward(lead, short_groups, source_b, lag_taps)
    up_second = [
        back_full[:, i : i + own].reshape(features, features)
        for i in range(0, own * up_blocks, own)
    ]
    place = own * up_blocks
    down_second = back_full[:, place : place + down_rows].reshape(hidden_width, features)
    place += down_rows
    proj_out = back_full[:, place : place + own].reshape(features, features)
    proj_gate = back_full[:, place + own :].reshape(features, features)
    gates = row_dot(normed2, proj_gate)
    gate_act = jax.nn.silu(gates)

    below = lambda v: jnp.pad(v, ((0, short_rows), (0, 0)))
    mixed = (mixed + below(at_home(carried))).astype(bf16).astype(f32)
    inputs_f = inputs_b.astype(f32)
    joined = mixed + gains[5] * inputs_f
    gated_b = (joined * gate_act).astype(bf16)

    residual2 = residual1 + row_dot(gated_b, proj_out)
    hat3, scale3 = norm(residual2)
    spread_b = (hat3 * gains[2]).astype(bf16) * valid_b
    rim = edges(spread_b[:long_rows], TILE)
    pre = conv_forward(lead, tap_count, short_groups, spread_b, rim, taps)
    residual3 = residual2 + jax.nn.silu(pre)
    ffn_second, kept_second = ffn_forward(residual3, gains[3], up_second, down_second)
    residual4 = residual3 + 0.5 * ffn_second
    hat5, scale5 = norm(residual4)
    final = (hat5 * gains[4]).astype(bf16)

    cotangent = jnp.concatenate([cotangent_long, cotangent_short], axis=0).astype(f32)
    grad4, grad_gain4 = norm_back(cotangent, gains[4], hat5, scale5)
    grad_b = (0.5 * grad4).astype(bf16)
    grad_hidden = hidden_grad(grad_b, kept_second, down_second)
    normed, _, active, hat, scale = kept_second
    by_owner = lambda g: g.astype(bf16).reshape(devices, -1, g.shape[1])
    piece, grad_gain3 = norm_back(back_through(grad_hidden, up_second), gains[3], hat, scale)
    grad3 = grad4 + piece
    grad_pre_b = (grad3 * silu_slope(pre)).astype(bf16)
    grad_pre_b, (normed, active) = tied(grad_pre_b, (normed, active))
    grad_rim = edges(grad_pre_b[:long_rows], TILE)
    second = Folding(
        [by_owner(inner_dot(normed, grad_hidden)), by_owner(inner_dot(active, grad_b))]
    )
    grad_pre_b = advance([second], grad_pre_b)
    grad_spread, small_rows = conv_backward(
        lead, tap_count, short_groups, grad_pre_b, grad_rim, spread_b, rim, taps
    )
    piece, grad_gain2 = norm_back(grad_spread * valid, gains[2], hat3, scale3)
    grad2 = grad3 + piece
    grad_out_b = advance([second], grad2.astype(bf16))
    grad_gated = outer_dot(grad_out_b, proj_out)
    grad_joined = grad_gated * gate_act
    grad_mixed_b = grad_joined.astype(bf16)
    grad_in, (grad_mixed_b, gated_b) = tied(
        to_owner(grad_mixed_b[:long_rows]), (grad_mixed_b, gated_b)
    )
    grad_in = at_owner(grad_in)
    grad_gates = grad_gated * joined * silu_slope(gates)
    grad_gain5 = jnp.sum(grad_joined * inputs_f, axis=0)
    grad_proj_out = by_owner(inner_dot(gated_b, grad_out_b))
    half = features // 2
    run = lambda grad, begin, into=None: mix_backward(
        lead, short_groups, grad, source_b, lag_flipped, begin, half, into
    )
    first_half = run(grad_mixed_b, 0)
    later = long_backward(grad_in, tables)
    later, grad_mixed_b = tied(later.astype(bf16), grad_mixed_b)
    later = from_owner(later)
    grad_mixed_b = advance([second], grad_mixed_b)
    grad_source, grad_lags = run(grad_mixed_b, 1, first_half)
    grad_source = (grad_source + below(at_home(later))).astype(bf16).astype(f32)
    grad_inner_b = (grad_source * valid + gains[5] * grad_joined).astype(bf16)
    grad_inner_b = advance([second], grad_inner_b)
    grad_gates_b = grad_gates.astype(bf16)
    back = outer_dot(grad_inner_b, proj_inner) + outer_dot(grad_gates_b, proj_gate)
    piece, grad_gain1 = norm_back(back, gains[1], hat2, scale2)
    grad1 = grad2 + piece
    grad_b = (0.5 * grad1).astype(bf16)
    normed, _, active, hat, scale = kept_first
    unit = (jnp.arange(LAGS)[:, None] == jnp.arange(features)[None, :]).astype(bf16)
    early_out = jnp.concatenate(
        [
            by_owner(inner_dot(normed2, grad_inner_b)),
            by_owner(inner_dot(normed2, grad_gates_b)),
            grad_proj_out,
            by_owner(inner_dot(grad_lags.astype(bf16), unit)),
        ],
        axis=1,
    )
    early = Folding([by_owner(inner_dot(active, grad_b)), early_out], 0)
    grad_b = advance([early], grad_b)
    grad_hidden = hidden_grad(grad_b, kept_first, down_first)
    grad_hidden = advance([second], grad_hidden)
    late = Folding([by_owner(inner_dot(normed, grad_hidden))], 0)
    grad_hidden = advance([late, early], grad_hidden)
    piece, grad_gain0 = norm_back(back_through(grad_hidden, up_first), gains[0], hat, scale)
    grad_zero_b = settle(second, advance([late], (grad1 + piece).astype(bf16)))

    row = jnp.arange(SMALL_ROWS)[:, None]
    gain_rows = [grad_gain0, grad_gain1, grad_gain2, grad_gain3, grad_gain4, grad_gain5]
    for k, grad_gain in enumerate(gain_rows):
        small_rows = jnp.where(row == k, grad_gain[None, :], small_rows)
    lane = jnp.arange(features)[None, :] - stem_width
    place = jnp.where(lane < gain_count, lane, lane - gain_count + TILE)
    small_unit = ((place == row) & (lane >= 0) & (lane < gain_count + tap_count)).astype(bf16)
    small_lanes = -(-(stem_width + gain_count + tap_count) // 128) * 128
    small = inner_dot(grad_zero_b, stacked) + inner_dot(small_rows.astype(bf16), small_unit)
    small = exchange(by_owner(small[:, :small_lanes]))
    grad_zero_b = advance([early], grad_zero_b)
    grad_stacked = row_dot(grad_zero_b, stem_full)[:, :stem_width]
    freq_float = freq_keep.astype(f32)
    time_float = time_keep.astype(f32)
    input_long = (
        grad_stacked[:long_rows].reshape(4 * long_rows, mel_bins) * freq_float[None, :]
    ).astype(bf16)
    input_short = (
        grad_stacked[long_rows:].reshape(4 * short_rows, mel_bins)
        * freq_float[None, :]
        * time_float[:, None]
    ).astype(bf16)
    input_long, input_short = advance([late], (input_long, input_short))
    for fold in (second, early):
        while not fold.done:
            advance([fold])
    moment_in, early.got = advance([late], ((long_in, grad_in, before), early.got))
    moment_in = settle(second, moment_in)
    moment, moment_slope = long_moments(*moment_in[:2], tables, moment_in[2], long_rows)
    sum_up2, sum_down2 = second.result()
    sum_early = early.result()
    grad_small = jnp.sum(small.astype(f32), axis=0)
    (sum_up1,) = late.result()
    sum_down1, rest = sum_early
    sum_in = jnp.concatenate([rest[:own], rest[own : 2 * own]], axis=1)
    sum_out = rest[2 * own : 3 * own]
    lag_grad = rest[3 * own :, :LAGS]

    states = log_rate.shape[1]
    steps = jnp.arange(LAGS).astype(f32)
    near = tuple(jnp.sum(lag_grad[:, None, :] * p, axis=2) for p in lag_powers)
    near_slope = tuple(jnp.sum((lag_grad * steps)[:, None, :] * p, axis=2) for p in lag_powers)
    shape = (own, states)
    moment = tuple(a.reshape(shape) + b for a, b in zip(moment, near))
    moment_slope = tuple(a.reshape(shape) + b for a, b in zip(moment_slope, near_slope))
    weight = tuple(w.reshape(shape) for w in tables["weight"])
    rate = tables["rate"].reshape(shape)
    scale = tables["scale"].reshape(shape)
    pulled = cmul(weight, moment)
    pulled_slope = cmul(weight, moment_slope)
    grad_rate = 0.5 * pulled[0] - rate * pulled_slope[0]
    grad_freq = -pulled_slope[1]
    grad_coef = jnp.concatenate([scale * moment[0], -scale * moment[1]], axis=1)

    return (
        final[:long_rows],
        final[long_rows:],
        input_long,
        input_short,
        grad_small[:, :stem_width],
        grad_small[:, stem_width : stem_width + gain_count],
        sum_up1,
        sum_down1,
        sum_in,
        sum_out,
        grad_rate,
        grad_freq,
        grad_coef,
        grad_small[:, stem_width + gain_count : stem_width + gain_count + tap_count],
        sum_up2,
        sum_down2,
    )


def solution(mesh):
    rows = P(AXES, None)
    flat = P(AXES)
    return jax.shard_map(
        local,
        mesh=mesh,
        in_specs=(rows, rows, P(), rows, flat, flat, flat, flat) + (rows,) * 14,
        out_specs=(rows,) * 16,
        check_vma=False,
    )
```

```python
from functools import partial

import jax
import jax.numpy as jnp
from jax import lax
from jax.experimental import pallas as pl
from jax.experimental.pallas import tpu as pltpu
from jax.sharding import PartitionSpec as P

GROUP = 32
LAGS = 192
TILE = 8
LANES = 256
SMALL_ROWS = 32
AXES = ("tm", "head")

f32 = jnp.float32
bf16 = jnp.bfloat16


def bits_of(axis):
    return (lax.axis_size(axis) - 1).bit_length()


def grid_of():
    tm, head = lax.axis_size("tm"), lax.axis_size("head")
    y = 1 << ((bits_of("tm") - 1) // 2)
    return tm // y, y, head // 2, 2


def places():
    _, y, x, _ = grid_of()
    names = [("tm", b) for b in reversed(range(y.bit_length() - 1))]
    return names + [("head", b) for b in reversed(range(bits_of("head")))]


def bit_order(first):
    heads = [n for n in places() if n[0] == "head" and n[1] > 0]
    tms = [n for n in places() if n[0] == "tm"]
    return heads + tms if first == "x" else tms + heads


def my_bit(name):
    return (lax.axis_index(name[0]) >> name[1]) & 1


def swap(value, name):
    axis, bit = name
    return lax.ppermute(value, axis, [(i, i ^ (1 << bit)) for i in range(lax.axis_size(axis))])


def send_along_z(value, hops):
    z, y, _, _ = grid_of()
    pairs = [(i, (i // y + hops) % z * y + i % y) for i in range(z * y)]
    return lax.ppermute(value, "tm", pairs)


def my_z():
    return lax.axis_index("tm") // grid_of()[1]


def joined_at(dim, mine, other, place):
    shape = mine.shape[:dim] + (2,) + mine.shape[dim:]
    index = lax.broadcasted_iota(jnp.int32, shape, dim)
    wide = lambda v: jnp.broadcast_to(jnp.expand_dims(v, dim), shape)
    return jnp.where(index == place, wide(mine), wide(other))


def tied(first, then):
    return lax.optimization_barrier((first, then))


def stacked_along_z(got):
    z = len(got)
    index = lax.broadcasted_iota(jnp.int32, (z,) + got[0].shape, 0)
    held = jnp.broadcast_to(got[0], index.shape)
    for hops in range(1, z):
        held = jnp.where(index == (my_z() - hops) % z, got[hops], held)
    return held


def pick(array, index):
    starts = [jnp.int32(0) if i is None else i for i in index]
    sizes = [n if i is None else 1 for n, i in zip(array.shape, index)]
    kept = [n for n, i in zip(array.shape, index) if i is None]
    tail = list(array.shape[len(index) :])
    starts += [jnp.int32(0)] * len(tail)
    return lax.dynamic_slice(array, starts, sizes + tail).reshape(kept + tail).astype(f32)


def settle(fold, values):
    newest, values = tied([terms[-1][0] for terms in fold.terms], values)
    for terms, array in zip(fold.terms, newest):
        terms[-1] = (array, terms[-1][1])
    return values


def all_bits():
    bits = [("tm", b) for b in reversed(range(bits_of("tm")))]
    return bits + [("head", b) for b in reversed(range(bits_of("head")))]


class Folding:
    last = None

    def __init__(self, grads, join=None):
        names = all_bits()
        self.high = [n for n in names if n[0] == "tm" and n not in places()]
        self.terms = [[(g.reshape((2,) * len(names) + g.shape[1:]), names)] for g in grads]
        firsts = "y" if len(grads) == 1 else "xy"
        self.todo = [[("head", 0)] + bit_order(first) for first in firsts]
        if join is None:
            self.todo = [todo + self.high[::-1] for todo in self.todo]
        self.fixed = [{} for _ in grads]
        self.join = join
        self.done = False

    def total(self, color, fixed):
        value = None
        for array, names in self.terms[color]:
            piece = pick(array, [fixed.get(name) for name in names])
            value = piece if value is None else value + piece
        return value

    def at_z(self, color, z):
        bits = {name: (z >> place) & 1 for place, name in enumerate(self.high[::-1])}
        return self.total(color, {**self.fixed[color], **bits})

    def load(self):
        if Folding.last is not None:
            newest = [terms[-1][0] for terms in self.terms]
            newest = tied(Folding.last, newest)[1]
            for terms, array in zip(self.terms, newest):
                terms[-1] = (array, terms[-1][1])
        colors = range(len(self.terms))
        values = []
        if self.todo[0]:
            for color in colors:
                name = self.todo[color][0]
                fixed = {**self.fixed[color], name: 1 - my_bit(name)}
                values.append(self.total(color, fixed).astype(bf16))
        elif self.join is not None:
            z = grid_of()[0]
            for hops in range(1, z):
                parts = [self.at_z(c, (my_z() + hops) % z).astype(bf16) for c in colors]
                values.append(jnp.concatenate(parts, axis=self.join))
        Folding.last = values or None
        return values

    def send(self, values):
        if self.todo[0]:
            for color, value in enumerate(values):
                name = self.todo[color].pop(0)
                got = swap(value, name)
                self.fixed[color][name] = my_bit(name)
                left = [n for n in all_bits() if n not in self.fixed[color]]
                self.terms[color].append((got, left))
        else:
            self.got = [send_along_z(v, hops + 1) for hops, v in enumerate(values)]
            self.done = True
        if self.join is None:
            self.done = not self.todo[0]

    def result(self):
        while not self.done:
            advance([self])
        if self.join is None:
            return [self.total(c, self.fixed[c]) for c in range(len(self.terms))]
        sums = [self.at_z(c, my_z()) for c in range(len(self.terms))]
        if len(sums) == 1:
            return [sums[0] + sum(got.astype(f32) for got in self.got)]
        cut = sums[0].shape[self.join]
        for got in self.got:
            pieces = (got[:cut], got[cut:]) if self.join == 0 else (got[:, :cut], got[:, cut:])
            sums = [a + b.astype(f32) for a, b in zip(sums, pieces)]
        return sums


def advance(folds, values=()):
    for fold in folds:
        if not fold.done:
            load = fold.load()
            values = tied(load, values)[1]
            fold.send(load)
    return values


def hold(fold, values):
    newest = tied(values, [terms[-1][0] for terms in fold.terms])[1]
    for terms, array in zip(fold.terms, newest):
        terms[-1] = (array, terms[-1][1])


def exchange(rows):
    return lax.all_to_all(rows, AXES, split_axis=0, concat_axis=0, tiled=True)


def edges(x, width):
    size = lax.axis_size("tm") * lax.axis_size("head")
    up = [(i, i + 1) for i in range(size - 1)]
    down = [(j, i) for i, j in up]
    before = lax.ppermute(x[x.shape[0] - width :], AXES, up)
    after = lax.ppermute(x[:width], AXES, down)
    return before, after


def row_dot(a, b):
    return jnp.dot(a, b, preferred_element_type=f32)


def inner_dot(a, b):
    return lax.dot_general(a, b, (((0,), (0,)), ((), ())), preferred_element_type=f32)


def outer_dot(a, b):
    return lax.dot_general(a, b, (((1,), (1,)), ((), ())), preferred_element_type=f32)


def norm(values):
    centred = values - jnp.mean(values, axis=-1, keepdims=True)
    scale = lax.rsqrt(jnp.mean(centred * centred, axis=-1, keepdims=True) + 1e-05)
    return centred * scale, scale


def norm_back(grad, gain, hat, scale):
    e = grad * gain
    back = e - jnp.mean(e, axis=-1, keepdims=True)
    back = (back - hat * jnp.mean(e * hat, axis=-1, keepdims=True)) * scale
    return back, jnp.sum(grad * hat, axis=0)


def silu_slope(values):
    logistic = jax.nn.sigmoid(values)
    return logistic * (1.0 + values * (1.0 - logistic))


def ffn_forward(residual, gain, up, down):
    hat, scale = norm(residual)
    normed = (hat * gain).astype(bf16)
    hidden = jnp.concatenate([row_dot(normed, part) for part in up], axis=1)
    active = jax.nn.silu(hidden).astype(bf16)
    return row_dot(active, down), (normed, hidden, active, hat, scale)


def column_blocks(x, width):
    return [x[:, i : i + width] for i in range(0, x.shape[1], width)]


def back_through(grad, parts):
    blocks = column_blocks(grad, grad.shape[1] // len(parts))
    return sum(outer_dot(block, part) for block, part in zip(blocks, parts))


def hidden_grad(grad_b, kept, down):
    return (outer_dot(grad_b, down) * silu_slope(kept[1])).astype(bf16)


def utterance_edges(groups, lead, blocks, block):
    first = jnp.int32(0)
    after = jnp.int32(lead)
    begin = jnp.int32(lead)
    for u in range(groups.shape[1]):
        end = begin + groups[0, u]
        inside = block >= begin
        first = jnp.where(inside, begin, first)
        after = jnp.where(inside, end, after)
        begin = end
    return first, after


def lag_tile(table, shift, tile):
    if isinstance(tile, int):
        return table[shift, tile * TILE : (tile + 1) * TILE, :]
    return table[shift, pl.ds(pl.multiple_of(tile * TILE, TILE), TILE), :]


def mix_forward_kernel(lead, groups, source, taps, out, rows_f, padded, table):
    blocks = source.shape[0] // GROUP
    tiles = GROUP // TILE
    rows_f[...] = source[...].astype(f32)
    padded[0:TILE, :] = jnp.zeros((TILE, padded.shape[1]), f32)
    padded[TILE:, :] = taps[...]
    for q in range(TILE):
        table[q] = padded[TILE - q : TILE - q + LAGS, :]

    def tile_of(ref, block, i):
        return ref[pl.ds(pl.multiple_of(block * GROUP + i * TILE, TILE), TILE), :]

    def one(block, carry):
        first, _ = utterance_edges(groups, lead, blocks, block)
        sums = [jnp.zeros((TILE, rows_f.shape[1]), f32) for _ in range(tiles)]
        own = [tile_of(rows_f, block, j) for j in range(tiles)]
        for q in range(TILE):
            lags = [lag_tile(table, q, d) for d in range(tiles)]
            for j in range(tiles):
                row = own[j][q : q + 1, :]
                for i in range(j, tiles):
                    sums[i] = sums[i] + lags[i - j] * row

        def pair(other, sums):
            sums = list(sums)
            base = (block - other) * tiles
            own = [tile_of(rows_f, other, j) for j in range(tiles)]
            for q in range(TILE):
                lags = {d: lag_tile(table, q, base + d) for d in range(1 - tiles, tiles)}
                for j in range(tiles):
                    row = own[j][q : q + 1, :]
                    for i in range(tiles):
                        sums[i] = sums[i] + lags[i - j] * row
            return tuple(sums)

        sums = lax.fori_loop(first, block, pair, tuple(sums))
        for i in range(tiles):
            out[pl.ds(pl.multiple_of(block * GROUP + i * TILE, TILE), TILE), :] = sums[i]
        return carry

    lax.fori_loop(0, blocks, one, 0)


def mix_backward_kernel(
    lead, groups, grad, source, taps_flipped, out, grad_taps, grad_f, rows_f, padded, table, sums_q
):
    blocks = source.shape[0] // GROUP
    tiles = GROUP // TILE
    top = LAGS // TILE - 1
    grad_f[...] = grad[...].astype(f32)
    rows_f[...] = source[...].astype(f32)
    padded[0:LAGS, :] = taps_flipped[...]
    padded[LAGS:, :] = jnp.zeros((TILE, padded.shape[1]), f32)
    for q in range(TILE):
        table[q] = padded[q : q + LAGS, :]
        sums_q[q] = jnp.zeros(sums_q.shape[1:], f32)

    def tile_of(ref, block, i):
        return ref[pl.ds(pl.multiple_of(block * GROUP + i * TILE, TILE), TILE), :]

    def add_to(q, tile, value):
        if isinstance(tile, int):
            place = slice(tile * TILE, (tile + 1) * TILE)
        else:
            place = pl.ds(pl.multiple_of(tile * TILE, TILE), TILE)
        sums_q[q, place, :] = sums_q[q, place, :] + value

    def one(block, carry):
        _, after = utterance_edges(groups, lead, blocks, block)
        sums = [jnp.zeros((TILE, rows_f.shape[1]), f32) for _ in range(tiles)]
        own = [tile_of(rows_f, block, j) for j in range(tiles)]
        here = [tile_of(grad_f, block, i) for i in range(tiles)]
        for q in range(TILE):
            lags = [lag_tile(table, TILE - 1 - q, top - d) for d in range(tiles)]
            for i in range(tiles):
                row = here[i][q : q + 1, :]
                for j in range(i + 1):
                    sums[j] = sums[j] + lags[i - j] * row
            rows = [own[j][q : q + 1, :] for j in range(tiles)]
            for d in range(tiles):
                total = here[d] * rows[0]
                for j in range(1, tiles - d):
                    total = total + here[d + j] * rows[j]
                add_to(q, d, total)

        def pair(other, sums):
            sums = list(sums)
            base = (other - block) * tiles
            here = [tile_of(grad_f, other, i) for i in range(tiles)]
            for q in range(TILE):
                lags = {
                    d: lag_tile(table, TILE - 1 - q, top - base - d)
                    for d in range(1 - tiles, tiles)
                }
                for i in range(tiles):
                    row = here[i][q : q + 1, :]
                    for j in range(tiles):
                        sums[j] = sums[j] + lags[i - j] * row
                rows = [own[j][q : q + 1, :] for j in range(tiles)]
                for d in range(1 - tiles, tiles):
                    total = None
                    for j in range(tiles):
                        if 0 <= j + d < tiles:
                            term = here[j + d] * rows[j]
                            total = term if total is None else total + term
                    add_to(q, base + d, total)
            return tuple(sums)

        sums = lax.fori_loop(block + 1, after, pair, tuple(sums))
        for j in range(tiles):
            out[pl.ds(pl.multiple_of(block * GROUP + j * TILE, TILE), TILE), :] = sums[j]
        return carry

    lax.fori_loop(0, blocks, one, 0)
    total = sums_q[0, 0:LAGS, :]
    for q in range(1, TILE):
        total = total + sums_q[q, q : q + LAGS, :]
    grad_taps[...] = total


def mixer_params():
    return pltpu.CompilerParams(vmem_limit_bytes=40 * 1024 * 1024)


def mix_forward(lead, groups, source, taps):
    rows, features = source.shape
    lanes = min(LANES, features)
    column = lambda count: pl.BlockSpec((count, lanes), lambda i: (0, i))
    return pl.pallas_call(
        partial(mix_forward_kernel, lead),
        out_shape=jax.ShapeDtypeStruct((rows, features), f32),
        grid=(features // lanes,),
        in_specs=[pl.BlockSpec(memory_space=pltpu.SMEM), column(rows), column(LAGS)],
        out_specs=column(rows),
        scratch_shapes=[
            pltpu.VMEM((rows, lanes), f32),
            pltpu.VMEM((LAGS + TILE, lanes), f32),
            pltpu.VMEM((TILE, LAGS, lanes), f32),
        ],
        compiler_params=mixer_params(),
        cost_estimate=pl.CostEstimate(
            flops=30000 * rows * features, bytes_accessed=rows * features * 8, transcendentals=0
        ),
        name="mix_forward",
    )(groups, source, taps)


def mix_backward(lead, groups, grad, source, taps_flipped, begin, width, into=None):
    rows, features = source.shape
    column = lambda count: pl.BlockSpec((count, width), lambda i: (0, begin))
    kept = [] if into is None else list(into)
    kernel = partial(mix_backward_kernel, lead)

    def body(*refs):
        kernel(*refs[:4], *refs[4 + len(kept) :])

    return pl.pallas_call(
        body,
        out_shape=(
            jax.ShapeDtypeStruct((rows, features), f32),
            jax.ShapeDtypeStruct((LAGS, features), f32),
        ),
        grid=(1,),
        in_specs=[
            pl.BlockSpec(memory_space=pltpu.SMEM),
            column(rows),
            column(rows),
            column(LAGS),
        ]
        + [pl.BlockSpec(memory_space=pl.ANY)] * len(kept),
        out_specs=(column(rows), column(LAGS)),
        scratch_shapes=[
            pltpu.VMEM((rows, width), f32),
            pltpu.VMEM((rows, width), f32),
            pltpu.VMEM((LAGS + TILE, width), f32),
            pltpu.VMEM((TILE, LAGS, width), f32),
            pltpu.VMEM((TILE, LAGS + TILE, width), f32),
        ],
        input_output_aliases={4 + i: i for i in range(len(kept))},
        compiler_params=mixer_params(),
        cost_estimate=pl.CostEstimate(
            flops=10000 * rows * width, bytes_accessed=rows * width * 8, transcendentals=0
        ),
        name="mix_backward",
    )(groups, grad, source, taps_flipped, *kept)


def fill_window(window, rows, before, after, lead, groups, block, blocks):
    first, stop = utterance_edges(groups, lead, blocks, block)
    place = lambda start, count: pl.ds(pl.multiple_of(start, 2 * TILE), count)
    window[TILE : TILE + GROUP, :] = rows[place(block * GROUP, GROUP), :].astype(f32)
    empty = jnp.zeros((TILE, window.shape[1]), f32)
    start = jnp.maximum(block * GROUP - 2 * TILE, 0)
    left = rows[place(start, 2 * TILE), :].astype(f32)[TILE:]
    left = jnp.where(block == 0, before[...].astype(f32), left)
    window[0:TILE, :] = jnp.where((block == 0) | (block > first), left, empty)
    start = jnp.minimum((block + 1) * GROUP, (blocks - 1) * GROUP)
    right = rows[place(start, 2 * TILE), :].astype(f32)[:TILE]
    right = jnp.where(block == lead - 1, after[...].astype(f32), right)
    keep = (block == lead - 1) | (block + 1 < stop)
    window[TILE + GROUP :, :] = jnp.where(keep, right, empty)


def conv_forward_kernel(lead, count, groups, rows, before, after, taps, out, window):
    blocks = rows.shape[0] // GROUP
    shift = TILE - count // 2

    def one(block, carry):
        fill_window(window, rows, before, after, lead, groups, block, blocks)
        total = None
        for k in range(count):
            term = window[shift + k : shift + k + GROUP, :] * taps[k : k + 1, :]
            total = term if total is None else total + term
        out[pl.ds(pl.multiple_of(block * GROUP, GROUP), GROUP), :] = total
        return carry

    lax.fori_loop(0, blocks, one, 0)


def conv_backward_kernel(
    lead, count, groups, grads, g_before, g_after, rows, before, after, taps, out, grad_taps,
    g_window, window, sums,
):
    blocks = rows.shape[0] // GROUP
    shift = TILE - count // 2
    sums[...] = jnp.zeros(sums.shape, f32)

    def one(block, carry):
        fill_window(g_window, grads, g_before, g_after, lead, groups, block, blocks)
        fill_window(window, rows, before, after, lead, groups, block, blocks)
        here = g_window[TILE : TILE + GROUP, :]
        total = None
        for k in range(count):
            lag = shift + count - 1 - k
            term = g_window[lag : lag + GROUP, :] * taps[k : k + 1, :]
            total = term if total is None else total + term
            product = here * window[shift + k : shift + k + GROUP, :]
            part = product[0:TILE]
            for i in range(TILE, GROUP, TILE):
                part = part + product[i : i + TILE]
            sums[k] = sums[k] + part
        out[pl.ds(pl.multiple_of(block * GROUP, GROUP), GROUP), :] = total
        return carry

    lax.fori_loop(0, blocks, one, 0)
    below = grad_taps.shape[0] - TILE - count
    grad_taps[...] = jnp.concatenate(
        [jnp.zeros((TILE, grad_taps.shape[1]), f32)]
        + [jnp.sum(sums[k], axis=0, keepdims=True) for k in range(count)]
        + [jnp.zeros((below, grad_taps.shape[1]), f32)],
        axis=0,
    )


def conv_call(kernel, lead, groups, arrays, outs, scratch, name):
    lanes = min(LANES, arrays[0].shape[1])
    column = lambda count: pl.BlockSpec((count, lanes), lambda i: (0, i))
    rows, features = arrays[0].shape
    return pl.pallas_call(
        kernel,
        out_shape=tuple(jax.ShapeDtypeStruct((n, features), f32) for n in outs),
        grid=(features // lanes,),
        in_specs=[pl.BlockSpec(memory_space=pltpu.SMEM)] + [column(a.shape[0]) for a in arrays],
        out_specs=tuple(column(n) for n in outs),
        scratch_shapes=[pltpu.VMEM(shape + (lanes,), f32) for shape in scratch],
        compiler_params=mixer_params(),
        cost_estimate=pl.CostEstimate(
            flops=4000 * rows * features, bytes_accessed=rows * features * 8, transcendentals=0
        ),
        name=name,
    )(groups, *arrays)


def conv_forward(lead, count, groups, rows, rim, taps):
    return conv_call(
        partial(conv_forward_kernel, lead, count),
        lead,
        groups,
        [rows, *rim, taps],
        [rows.shape[0]],
        [(GROUP + 2 * TILE,)],
        "conv_forward",
    )[0]


def conv_backward(lead, count, groups, grads, g_rim, rows, rim, taps):
    return conv_call(
        partial(conv_backward_kernel, lead, count),
        lead,
        groups,
        [grads, *g_rim, rows, *rim, taps],
        [rows.shape[0], SMALL_ROWS],
        [(GROUP + 2 * TILE,), (GROUP + 2 * TILE,), (count, TILE)],
        "conv_backward",
    )


def stack_rows(pieces, lanes):
    pieces = list(pieces)
    if any(p.shape[0] % 16 for p in pieces):
        fill = lambda p: jnp.pad(p, ((0, 0), (0, lanes - p.shape[1])))
        blocks = [b for p in pieces for b in (column_blocks(p, lanes) if p.shape[1] > lanes else [p])]
        return jnp.concatenate([fill(b) for b in blocks], axis=0)
    total = sum(p.shape[0] * -(-p.shape[1] // lanes) for p in pieces)

    def kernel(*refs):
        out, row = refs[-1], 0
        for ref in refs[:-1]:
            count, width = ref.shape
            for begin in range(0, width, lanes):
                here = min(lanes, width - begin)
                if here < lanes:
                    out[row : row + count, :] = jnp.zeros((count, lanes), out.dtype)
                out[row : row + count, 0:here] = ref[:, begin : begin + here]
                row += count

    return pl.pallas_call(
        kernel,
        out_shape=jax.ShapeDtypeStruct((total, lanes), pieces[0].dtype),
        in_specs=[pl.BlockSpec(memory_space=pltpu.VMEM)] * len(pieces),
        out_specs=pl.BlockSpec(memory_space=pltpu.VMEM),
        compiler_params=mixer_params(),
        name="stack_rows",
    )(*pieces)


def cmul(a, b):
    return (a[0] * b[0] - a[1] * b[1], a[0] * b[1] + a[1] * b[0])


def powers(rate, freq, steps):
    decay = jnp.exp(-rate * steps)
    return decay * jnp.cos(freq * steps), decay * jnp.sin(freq * steps)


def shifted(x, count):
    pad = jnp.zeros((abs(count),) + x.shape[1:], x.dtype)
    if count > 0:
        return jnp.concatenate([pad, x[:-count]], axis=0)
    return jnp.concatenate([x[-count:], pad], axis=0)


def chunk_scan(values, decay, sign):
    count = values[0].shape[0]
    hop = 1
    while hop < count:
        moved = tuple(shifted(v, sign * hop) for v in values)
        added = cmul(decay, moved)
        values = (values[0] + added[0], values[1] + added[1])
        decay = cmul(decay, decay)
        hop *= 2
    return values


def long_tables(log_rate, freq, coef, chunk):
    channels, states = log_rate.shape
    lanes = channels * states
    rate = jnp.exp(log_rate).reshape(1, lanes)
    freq = freq.reshape(1, lanes)
    scale = jnp.sqrt(2.0 * rate)
    weight = (
        scale * coef[:, :states].reshape(1, lanes),
        scale * coef[:, states:].reshape(1, lanes),
    )
    steps = jnp.arange(chunk + 1).astype(f32)[:, None]
    power = powers(rate, freq, steps)
    mask = jnp.arange(channels)[:, None] == (jnp.arange(lanes) // states)[None, :]
    mask = mask.astype(f32)[:, None, :]

    def spread(pair):
        wide = [(mask * part[None]).reshape(channels * chunk, lanes) for part in pair]
        return jnp.concatenate(wide, axis=1).astype(bf16)

    ages = tuple(p[:chunk][::-1] for p in power)
    leads = tuple(p[1:] for p in power)
    weighted = lambda pair: cmul(weight, pair)
    signed = lambda pair: (pair[0], -pair[1])
    return {
        "ages": spread(ages),
        "ages_slope": spread(tuple(a * steps[:chunk][::-1] for a in ages)),
        "leads": spread(leads),
        "leads_slope": spread(tuple(a * steps[1:] for a in leads)),
        "read": spread(signed(weighted(leads))),
        "read_back": spread(signed(weighted(ages))),
        "decay": powers(rate, freq, jnp.float32(chunk)),
        "rate": rate,
        "scale": scale,
        "weight": weight,
    }


def halves(x):
    lanes = x.shape[1] // 2
    return x[:, :lanes], x[:, lanes:]


def long_forward(rows, tables):
    added = halves(row_dot(rows, tables["ages"]))
    state = chunk_scan(added, tables["decay"], 1)
    before = tuple(shifted(v, 1) for v in state)
    carried = outer_dot(jnp.concatenate(before, axis=1).astype(bf16), tables["read"])
    return carried, before


def long_backward(grads, tables):
    read = halves(row_dot(grads, tables["leads"]))
    future = chunk_scan(read, tables["decay"], -1)
    later = tuple(shifted(v, -1) for v in future)
    return outer_dot(jnp.concatenate(later, axis=1).astype(bf16), tables["read_back"])


def long_moments(rows, grads, tables, before, chunk):
    added = halves(row_dot(rows, tables["ages_slope"]))
    late = cmul(tables["decay"], before)
    added = tuple(a + chunk * b for a, b in zip(added, late))
    slope_before = tuple(shifted(v, 1) for v in chunk_scan(added, tables["decay"], 1))
    read = halves(row_dot(grads, tables["leads"]))
    slope = halves(row_dot(grads, tables["leads_slope"]))
    total = lambda pair: tuple(jnp.sum(v, axis=0, keepdims=True) for v in pair)
    moment = total(cmul(read, before))
    first = cmul(slope, before)
    second = cmul(read, slope_before)
    return moment, total((first[0] + second[0], first[1] + second[1]))


def lag_values(log_rate, freq, coef, lags):
    states = log_rate.shape[1]
    rate = jnp.exp(log_rate)
    scale = jnp.sqrt(2.0 * rate)
    steps = jnp.arange(lags).astype(f32)
    real, imaginary = powers(rate[:, :, None], freq[:, :, None], steps)
    weights = (scale * coef[:, :states], scale * coef[:, states:])
    taps = jnp.sum(weights[0][:, :, None] * real - weights[1][:, :, None] * imaginary, axis=1)
    return taps, (real, imaginary)


def local(*args):
    Folding.last = None
    return layer(*args)


def layer(
    feats_long,
    feats_short,
    long_length,
    short_groups,
    freq_start,
    freq_width,
    time_start,
    time_width,
    stem_weight,
    norm_gains,
    ffn1_up,
    ffn1_down,
    mixer_in,
    mixer_out,
    mixer_log_rate,
    mixer_freq,
    mixer_coef,
    conv_taps,
    ffn2_up,
    ffn2_down,
    cotangent_long,
    cotangent_short,
):
    devices = lax.axis_size("tm") * lax.axis_size("head")
    own = stem_weight.shape[0]
    features = own * devices
    hidden_width = ffn1_up.shape[1]
    mel_bins = feats_long.shape[1]
    stem_width = stem_weight.shape[1]
    gain_count, tap_count = norm_gains.shape[1], conv_taps.shape[1]
    down_rows = ffn1_down.shape[0]
    up_blocks = hidden_width // features
    long_rows = feats_long.shape[0] // 4
    short_rows = feats_short.shape[0] // 4
    lead = long_rows // GROUP
    padded_to = lambda w, lanes: jnp.pad(w, ((0, 0), (0, lanes - w.shape[1])))

    block = stack_rows(
        [ffn1_up, mixer_in[:, :features], ffn1_down, stem_weight], features
    )
    split = own * (up_blocks + 1)
    got = [block] + [send_along_z(block, hops) for hops in range(1, grid_of()[0])]
    held = [
        stacked_along_z([g[:split] for g in got]),
        stacked_along_z([g[split:] for g in got]),
    ]
    back = stack_rows([ffn2_up, ffn2_down, mixer_out, mixer_in[:, features:]], features)

    held, mixer_params_own = tied(held, (mixer_log_rate, mixer_freq, mixer_coef))
    log_rate, freq_values, coef_values = (p.astype(f32) for p in mixer_params_own)
    own_taps, lag_powers = lag_values(log_rate, freq_values, coef_values, LAGS)
    shared = jnp.concatenate([own_taps.astype(bf16), norm_gains, conv_taps], axis=1)
    shared = padded_to(shared, -(-shared.shape[1] // 128) * 128)
    shared = exchange(jnp.broadcast_to(shared, (devices,) + shared.shape))

    dims = [[], []]
    orders = [bit_order("x"), bit_order("y")]
    tables_in = (log_rate, freq_values, coef_values)
    for step in range(len(orders[0])):
        for color in range(2):
            name = orders[color][step]
            other = swap(held[color], name)
            dims[color] = [n for n in places() if n in dims[color] or n == name]
            held[color] = joined_at(
                1 + dims[color].index(name), held[color], other, my_bit(name)
            )
        if step == 0:
            held, (tables_in, back) = tied(held, (tables_in, back))
    back_full = lax.all_gather(back, AXES, axis=0)
    mel_index = jnp.arange(mel_bins)
    mel_band = (mel_index >= freq_start[0]) & (mel_index < freq_start[0] + freq_width[0])
    freq_keep = (1 - mel_band.astype(jnp.int32)).astype(bf16)
    row_index = jnp.arange(4 * short_rows)
    time_blank = (row_index >= time_start[0]) & (row_index < time_start[0] + time_width[0])
    time_keep = (1 - time_blank.astype(jnp.int32)).astype(bf16)
    stacked = jnp.concatenate(
        [
            (feats_long * freq_keep[None, :]).reshape(long_rows, 4 * mel_bins),
            (feats_short * freq_keep[None, :] * time_keep[:, None]).reshape(
                short_rows, 4 * mel_bins
            ),
        ],
        axis=0,
    )
    stacked = padded_to(stacked, features)
    tables = long_tables(*tables_in, long_rows)
    shared = shared.reshape(features, -1).astype(f32).T
    held, (tables["ages"], shared, stacked) = tied(held, (tables["ages"], shared, stacked))
    core = ("head", 0)
    other = [swap(h, core) for h in held]

    def assembled(color, begin, count, lanes=features):
        part = lambda v: v[..., begin : begin + count, :lanes]
        full = joined_at(1 + len(dims[color]), part(held[color]), part(other[color]), my_bit(core))
        return full.reshape(-1, lanes)

    up_first = [assembled(0, i * own, own) for i in range(up_blocks)]
    proj_inner = assembled(0, up_blocks * own, own)
    down_first = assembled(1, 0, down_rows)
    stem_full = assembled(1, down_rows, own)

    lag_taps = shared[:LAGS]
    lag_flipped = lag_taps[::-1]
    gains = shared[LAGS : LAGS + gain_count]
    taps = padded_to(shared[LAGS + gain_count : LAGS + gain_count + tap_count].T, 16).T

    position = lax.axis_index(AXES) * long_rows + jnp.arange(long_rows)
    valid_long = (position < long_length[0]).astype(f32)
    valid = jnp.concatenate([valid_long, jnp.ones((short_rows,), f32)])[:, None]
    valid_b = valid.astype(bf16)

    residual = outer_dot(stacked, stem_full)
    ffn_first, kept_first = ffn_forward(residual, gains[0], up_first, down_first)
    residual1 = residual + 0.5 * ffn_first
    hat2, scale2 = norm(residual1)
    normed2 = (hat2 * gains[1]).astype(bf16)
    inputs_b = row_dot(normed2, proj_inner).astype(bf16)
    source_b = inputs_b * valid_b

    def to_owner(rows):
        return rows.T.reshape(devices, 8, own * long_rows // 8)

    def at_owner(rows):
        return exchange(rows).reshape(devices, own * long_rows)

    def from_owner(rows):
        return exchange(rows.astype(bf16).reshape(devices, 8, own * long_rows // 8))

    def at_home(rows):
        return rows.reshape(features, long_rows).T.astype(f32)

    long_in, normed2 = tied(to_owner(source_b[:long_rows]), normed2)
    long_in = at_owner(long_in)
    carried, before = long_forward(long_in, tables)
    carried, source_b = tied(carried.astype(bf16), source_b)
    carried = from_owner(carried)
    mixed = mix_forward(lead, short_groups, source_b, lag_taps)
    up_second = [
        back_full[:, i : i + own].reshape(features, features)
        for i in range(0, own * up_blocks, own)
    ]
    place = own * up_blocks
    down_second = back_full[:, place : place + down_rows].reshape(hidden_width, features)
    place += down_rows
    proj_out = back_full[:, place : place + own].reshape(features, features)
    proj_gate = back_full[:, place + own :].reshape(features, features)
    gates = row_dot(normed2, proj_gate)
    gate_act = jax.nn.silu(gates)

    below = lambda v: jnp.pad(v, ((0, short_rows), (0, 0)))
    mixed = (mixed + below(at_home(carried))).astype(bf16).astype(f32)
    inputs_f = inputs_b.astype(f32)
    joined = mixed + gains[5] * inputs_f
    gated_b = (joined * gate_act).astype(bf16)

    residual2 = residual1 + row_dot(gated_b, proj_out)
    hat3, scale3 = norm(residual2)
    spread_b = (hat3 * gains[2]).astype(bf16) * valid_b
    rim = edges(spread_b[:long_rows], TILE)
    pre = conv_forward(lead, tap_count, short_groups, spread_b, rim, taps)
    residual3 = residual2 + jax.nn.silu(pre)
    ffn_second, kept_second = ffn_forward(residual3, gains[3], up_second, down_second)
    residual4 = residual3 + 0.5 * ffn_second
    hat5, scale5 = norm(residual4)
    final = (hat5 * gains[4]).astype(bf16)

    cotangent = jnp.concatenate([cotangent_long, cotangent_short], axis=0).astype(f32)
    grad4, grad_gain4 = norm_back(cotangent, gains[4], hat5, scale5)
    grad_b = (0.5 * grad4).astype(bf16)
    grad_hidden = hidden_grad(grad_b, kept_second, down_second)
    normed, _, active, hat, scale = kept_second
    by_owner = lambda g: g.astype(bf16).reshape(devices, -1, g.shape[1])
    piece, grad_gain3 = norm_back(back_through(grad_hidden, up_second), gains[3], hat, scale)
    grad3 = grad4 + piece
    grad_pre_b = (grad3 * silu_slope(pre)).astype(bf16)
    grad_pre_b, (normed, active) = tied(grad_pre_b, (normed, active))
    grad_rim = edges(grad_pre_b[:long_rows], TILE)
    second = Folding(
        [by_owner(inner_dot(normed, grad_hidden)), by_owner(inner_dot(active, grad_b))]
    )
    grad_pre_b = advance([second], grad_pre_b)
    grad_spread, small_rows = conv_backward(
        lead, tap_count, short_groups, grad_pre_b, grad_rim, spread_b, rim, taps
    )
    piece, grad_gain2 = norm_back(grad_spread * valid, gains[2], hat3, scale3)
    grad2 = grad3 + piece
    grad_out_b = advance([second], grad2.astype(bf16))
    grad_gated = outer_dot(grad_out_b, proj_out)
    grad_joined = grad_gated * gate_act
    grad_mixed_b = grad_joined.astype(bf16)
    grad_in, (grad_mixed_b, gated_b) = tied(
        to_owner(grad_mixed_b[:long_rows]), (grad_mixed_b, gated_b)
    )
    grad_in = at_owner(grad_in)
    grad_gates = grad_gated * joined * silu_slope(gates)
    grad_gain5 = jnp.sum(grad_joined * inputs_f, axis=0)
    grad_proj_out = by_owner(inner_dot(gated_b, grad_out_b))
    half = features // 2
    run = lambda grad, begin, into=None: mix_backward(
        lead, short_groups, grad, source_b, lag_flipped, begin, half, into
    )
    first_half = run(grad_mixed_b, 0)
    later = long_backward(grad_in, tables)
    later, grad_mixed_b = tied(later.astype(bf16), grad_mixed_b)
    later = from_owner(later)
    grad_mixed_b = advance([second], grad_mixed_b)
    grad_source, grad_lags = run(grad_mixed_b, 1, first_half)
    grad_source = (grad_source + below(at_home(later))).astype(bf16).astype(f32)
    grad_inner_b = (grad_source * valid + gains[5] * grad_joined).astype(bf16)
    grad_inner_b = advance([second], grad_inner_b)
    grad_gates_b = grad_gates.astype(bf16)
    back = outer_dot(grad_inner_b, proj_inner) + outer_dot(grad_gates_b, proj_gate)
    piece, grad_gain1 = norm_back(back, gains[1], hat2, scale2)
    grad1 = grad2 + piece
    grad_b = (0.5 * grad1).astype(bf16)
    normed, _, active, hat, scale = kept_first
    unit = (jnp.arange(LAGS)[:, None] == jnp.arange(features)[None, :]).astype(bf16)
    early_out = jnp.concatenate(
        [
            by_owner(inner_dot(normed2, grad_inner_b)),
            by_owner(inner_dot(normed2, grad_gates_b)),
            grad_proj_out,
            by_owner(inner_dot(grad_lags.astype(bf16), unit)),
        ],
        axis=1,
    )
    early = Folding([by_owner(inner_dot(active, grad_b)), early_out], 0)
    grad_b = advance([early], grad_b)
    grad_hidden = hidden_grad(grad_b, kept_first, down_first)
    grad_hidden = advance([second], grad_hidden)
    late = Folding([by_owner(inner_dot(normed, grad_hidden))], 0)
    grad_hidden = advance([late, early], grad_hidden)
    piece, grad_gain0 = norm_back(back_through(grad_hidden, up_first), gains[0], hat, scale)
    grad_zero_b = settle(second, advance([late], (grad1 + piece).astype(bf16)))

    row = jnp.arange(SMALL_ROWS)[:, None]
    gain_rows = [grad_gain0, grad_gain1, grad_gain2, grad_gain3, grad_gain4, grad_gain5]
    for k, grad_gain in enumerate(gain_rows):
        small_rows = jnp.where(row == k, grad_gain[None, :], small_rows)
    lane = jnp.arange(features)[None, :] - stem_width
    place = jnp.where(lane < gain_count, lane, lane - gain_count + TILE)
    small_unit = ((place == row) & (lane >= 0) & (lane < gain_count + tap_count)).astype(bf16)
    small_lanes = -(-(stem_width + gain_count + tap_count) // 128) * 128
    small = inner_dot(grad_zero_b, stacked) + inner_dot(small_rows.astype(bf16), small_unit)
    small = exchange(by_owner(small[:, :small_lanes]))
    grad_zero_b = advance([early], grad_zero_b)
    grad_stacked = row_dot(grad_zero_b, stem_full)[:, :stem_width]
    freq_float = freq_keep.astype(f32)
    time_float = time_keep.astype(f32)
    input_long = (
        grad_stacked[:long_rows].reshape(4 * long_rows, mel_bins) * freq_float[None, :]
    ).astype(bf16)
    input_short = (
        grad_stacked[long_rows:].reshape(4 * short_rows, mel_bins)
        * freq_float[None, :]
        * time_float[:, None]
    ).astype(bf16)
    while not second.done:
        advance([second])
    sum_up2, sum_down2 = second.result()
    hold(late, (sum_up2, sum_down2))
    input_long, input_short = advance([late], (input_long, input_short))
    while not early.done:
        advance([early])
    moment_in = advance([late], (long_in, grad_in, before))
    moment, moment_slope = long_moments(*moment_in[:2], tables, moment_in[2], long_rows)
    sum_early = early.result()
    grad_small = jnp.sum(small.astype(f32), axis=0)
    (sum_up1,) = late.result()
    sum_down1, rest = sum_early
    sum_in = jnp.concatenate([rest[:own], rest[own : 2 * own]], axis=1)
    sum_out = rest[2 * own : 3 * own]
    lag_grad = rest[3 * own :, :LAGS]

    states = log_rate.shape[1]
    steps = jnp.arange(LAGS).astype(f32)
    near = tuple(jnp.sum(lag_grad[:, None, :] * p, axis=2) for p in lag_powers)
    near_slope = tuple(jnp.sum((lag_grad * steps)[:, None, :] * p, axis=2) for p in lag_powers)
    shape = (own, states)
    moment = tuple(a.reshape(shape) + b for a, b in zip(moment, near))
    moment_slope = tuple(a.reshape(shape) + b for a, b in zip(moment_slope, near_slope))
    weight = tuple(w.reshape(shape) for w in tables["weight"])
    rate = tables["rate"].reshape(shape)
    scale = tables["scale"].reshape(shape)
    pulled = cmul(weight, moment)
    pulled_slope = cmul(weight, moment_slope)
    grad_rate = 0.5 * pulled[0] - rate * pulled_slope[0]
    grad_freq = -pulled_slope[1]
    grad_coef = jnp.concatenate([scale * moment[0], -scale * moment[1]], axis=1)

    return (
        final[:long_rows],
        final[long_rows:],
        input_long,
        input_short,
        grad_small[:, :stem_width],
        grad_small[:, stem_width : stem_width + gain_count],
        sum_up1,
        sum_down1,
        sum_in,
        sum_out,
        grad_rate,
        grad_freq,
        grad_coef,
        grad_small[:, stem_width + gain_count : stem_width + gain_count + tap_count],
        sum_up2,
        sum_down2,
    )


def solution(mesh):
    rows = P(AXES, None)
    flat = P(AXES)
    return jax.shard_map(
        local,
        mesh=mesh,
        in_specs=(rows, rows, P(), rows, flat, flat, flat, flat) + (rows,) * 14,
        out_specs=(rows,) * 16,
        check_vma=False,
    )
```

```python
from functools import partial

import jax
import jax.numpy as jnp
from jax import lax
from jax.experimental import pallas as pl
from jax.experimental.pallas import tpu as pltpu
from jax.sharding import PartitionSpec as P

GROUP = 32
LAGS = 192
TILE = 8
LANES = 256
SMALL_ROWS = 32
AXES = ("tm", "head")

f32 = jnp.float32
bf16 = jnp.bfloat16


def bits_of(axis):
    return (lax.axis_size(axis) - 1).bit_length()


def grid_of():
    tm, head = lax.axis_size("tm"), lax.axis_size("head")
    y = 1 << ((bits_of("tm") - 1) // 2)
    return tm // y, y, head // 2, 2


def places():
    _, y, x, _ = grid_of()
    names = [("tm", b) for b in reversed(range(y.bit_length() - 1))]
    return names + [("head", b) for b in reversed(range(bits_of("head")))]


def bit_order(first):
    heads = [n for n in places() if n[0] == "head" and n[1] > 0]
    tms = [n for n in places() if n[0] == "tm"]
    return heads + tms if first == "x" else tms + heads


def my_bit(name):
    return (lax.axis_index(name[0]) >> name[1]) & 1


def swap(value, name):
    axis, bit = name
    return lax.ppermute(value, axis, [(i, i ^ (1 << bit)) for i in range(lax.axis_size(axis))])


def send_along_z(value, hops):
    z, y, _, _ = grid_of()
    pairs = [(i, (i // y + hops) % z * y + i % y) for i in range(z * y)]
    return lax.ppermute(value, "tm", pairs)


def my_z():
    return lax.axis_index("tm") // grid_of()[1]


def joined_at(dim, mine, other, place):
    shape = mine.shape[:dim] + (2,) + mine.shape[dim:]
    index = lax.broadcasted_iota(jnp.int32, shape, dim)
    wide = lambda v: jnp.broadcast_to(jnp.expand_dims(v, dim), shape)
    return jnp.where(index == place, wide(mine), wide(other))


def tied(first, then):
    return lax.optimization_barrier((first, then))


def stacked_along_z(got):
    z = len(got)
    index = lax.broadcasted_iota(jnp.int32, (z,) + got[0].shape, 0)
    held = jnp.broadcast_to(got[0], index.shape)
    for hops in range(1, z):
        held = jnp.where(index == (my_z() - hops) % z, got[hops], held)
    return held


def pick(array, index):
    starts = [jnp.int32(0) if i is None else i for i in index]
    sizes = [n if i is None else 1 for n, i in zip(array.shape, index)]
    kept = [n for n, i in zip(array.shape, index) if i is None]
    tail = list(array.shape[len(index) :])
    starts += [jnp.int32(0)] * len(tail)
    return lax.dynamic_slice(array, starts, sizes + tail).reshape(kept + tail).astype(f32)


def settle(fold, values):
    newest, values = tied([terms[-1][0] for terms in fold.terms], values)
    for terms, array in zip(fold.terms, newest):
        terms[-1] = (array, terms[-1][1])
    return values


def all_bits():
    bits = [("tm", b) for b in reversed(range(bits_of("tm")))]
    return bits + [("head", b) for b in reversed(range(bits_of("head")))]


class Folding:
    last = None

    def __init__(self, grads, join=None):
        names = all_bits()
        self.high = [n for n in names if n[0] == "tm" and n not in places()]
        self.terms = [[(g.reshape((2,) * len(names) + g.shape[1:]), names)] for g in grads]
        firsts = "y" if len(grads) == 1 else "xy"
        self.todo = [[("head", 0)] + bit_order(first) for first in firsts]
        if join is None:
            self.todo = [todo + self.high[::-1] for todo in self.todo]
        self.fixed = [{} for _ in grads]
        self.join = join
        self.done = False

    def total(self, color, fixed):
        value = None
        for array, names in self.terms[color]:
            piece = pick(array, [fixed.get(name) for name in names])
            value = piece if value is None else value + piece
        return value

    def at_z(self, color, z):
        bits = {name: (z >> place) & 1 for place, name in enumerate(self.high[::-1])}
        return self.total(color, {**self.fixed[color], **bits})

    def load(self):
        if Folding.last is not None:
            newest = [terms[-1][0] for terms in self.terms]
            newest = tied(Folding.last, newest)[1]
            for terms, array in zip(self.terms, newest):
                terms[-1] = (array, terms[-1][1])
        colors = range(len(self.terms))
        values = []
        if self.todo[0]:
            for color in colors:
                name = self.todo[color][0]
                fixed = {**self.fixed[color], name: 1 - my_bit(name)}
                values.append(self.total(color, fixed).astype(bf16))
        elif self.join is not None:
            z = grid_of()[0]
            for hops in range(1, z):
                parts = [self.at_z(c, (my_z() + hops) % z).astype(bf16) for c in colors]
                values.append(jnp.concatenate(parts, axis=self.join))
        Folding.last = values or None
        return values

    def send(self, values):
        if self.todo[0]:
            for color, value in enumerate(values):
                name = self.todo[color].pop(0)
                got = swap(value, name)
                self.fixed[color][name] = my_bit(name)
                left = [n for n in all_bits() if n not in self.fixed[color]]
                self.terms[color].append((got, left))
        else:
            self.got = [send_along_z(v, hops + 1) for hops, v in enumerate(values)]
            self.done = True
        if self.join is None:
            self.done = not self.todo[0]

    def result(self):
        while not self.done:
            advance([self])
        if self.join is None:
            return [self.total(c, self.fixed[c]) for c in range(len(self.terms))]
        sums = [self.at_z(c, my_z()) for c in range(len(self.terms))]
        if len(sums) == 1:
            return [sums[0] + sum(got.astype(f32) for got in self.got)]
        cut = sums[0].shape[self.join]
        for got in self.got:
            pieces = (got[:cut], got[cut:]) if self.join == 0 else (got[:, :cut], got[:, cut:])
            sums = [a + b.astype(f32) for a, b in zip(sums, pieces)]
        return sums


def advance(folds, values=()):
    for fold in folds:
        if not fold.done:
            load = fold.load()
            values = tied(load, values)[1]
            fold.send(load)
    return values


def hold(fold, values):
    newest = tied(values, [terms[-1][0] for terms in fold.terms])[1]
    for terms, array in zip(fold.terms, newest):
        terms[-1] = (array, terms[-1][1])


def exchange(rows):
    return lax.all_to_all(rows, AXES, split_axis=0, concat_axis=0, tiled=True)


def edges(x, width):
    size = lax.axis_size("tm") * lax.axis_size("head")
    up = [(i, i + 1) for i in range(size - 1)]
    down = [(j, i) for i, j in up]
    before = lax.ppermute(x[x.shape[0] - width :], AXES, up)
    after = lax.ppermute(x[:width], AXES, down)
    return before, after


def row_dot(a, b):
    return jnp.dot(a, b, preferred_element_type=f32)


def inner_dot(a, b):
    return lax.dot_general(a, b, (((0,), (0,)), ((), ())), preferred_element_type=f32)


def outer_dot(a, b):
    return lax.dot_general(a, b, (((1,), (1,)), ((), ())), preferred_element_type=f32)


def norm(values):
    centred = values - jnp.mean(values, axis=-1, keepdims=True)
    scale = lax.rsqrt(jnp.mean(centred * centred, axis=-1, keepdims=True) + 1e-05)
    return centred * scale, scale


def norm_back(grad, gain, hat, scale):
    e = grad * gain
    back = e - jnp.mean(e, axis=-1, keepdims=True)
    back = (back - hat * jnp.mean(e * hat, axis=-1, keepdims=True)) * scale
    return back, jnp.sum(grad * hat, axis=0)


def silu_slope(values):
    logistic = jax.nn.sigmoid(values)
    return logistic * (1.0 + values * (1.0 - logistic))


def ffn_forward(residual, gain, up, down):
    hat, scale = norm(residual)
    normed = (hat * gain).astype(bf16)
    hidden = jnp.concatenate([row_dot(normed, part) for part in up], axis=1)
    active = jax.nn.silu(hidden).astype(bf16)
    return row_dot(active, down), (normed, hidden, active, hat, scale)


def column_blocks(x, width):
    return [x[:, i : i + width] for i in range(0, x.shape[1], width)]


def back_through(grad, parts):
    blocks = column_blocks(grad, grad.shape[1] // len(parts))
    return sum(outer_dot(block, part) for block, part in zip(blocks, parts))


def hidden_grad(grad_b, kept, down):
    return (outer_dot(grad_b, down) * silu_slope(kept[1])).astype(bf16)


def utterance_edges(groups, lead, blocks, block):
    first = jnp.int32(0)
    after = jnp.int32(lead)
    begin = jnp.int32(lead)
    for u in range(groups.shape[1]):
        end = begin + groups[0, u]
        inside = block >= begin
        first = jnp.where(inside, begin, first)
        after = jnp.where(inside, end, after)
        begin = end
    return first, after


def lag_tile(table, shift, tile):
    if isinstance(tile, int):
        return table[shift, tile * TILE : (tile + 1) * TILE, :]
    return table[shift, pl.ds(pl.multiple_of(tile * TILE, TILE), TILE), :]


def mix_forward_kernel(lead, groups, source, taps, out, rows_f, padded, table):
    blocks = source.shape[0] // GROUP
    tiles = GROUP // TILE
    rows_f[...] = source[...].astype(f32)
    padded[0:TILE, :] = jnp.zeros((TILE, padded.shape[1]), f32)
    padded[TILE:, :] = taps[...]
    for q in range(TILE):
        table[q] = padded[TILE - q : TILE - q + LAGS, :]

    def tile_of(ref, block, i):
        return ref[pl.ds(pl.multiple_of(block * GROUP + i * TILE, TILE), TILE), :]

    def one(block, carry):
        first, _ = utterance_edges(groups, lead, blocks, block)
        sums = [jnp.zeros((TILE, rows_f.shape[1]), f32) for _ in range(tiles)]
        own = [tile_of(rows_f, block, j) for j in range(tiles)]
        for q in range(TILE):
            lags = [lag_tile(table, q, d) for d in range(tiles)]
            for j in range(tiles):
                row = own[j][q : q + 1, :]
                for i in range(j, tiles):
                    sums[i] = sums[i] + lags[i - j] * row

        def pair(other, sums):
            sums = list(sums)
            base = (block - other) * tiles
            own = [tile_of(rows_f, other, j) for j in range(tiles)]
            for q in range(TILE):
                lags = {d: lag_tile(table, q, base + d) for d in range(1 - tiles, tiles)}
                for j in range(tiles):
                    row = own[j][q : q + 1, :]
                    for i in range(tiles):
                        sums[i] = sums[i] + lags[i - j] * row
            return tuple(sums)

        sums = lax.fori_loop(first, block, pair, tuple(sums))
        for i in range(tiles):
            out[pl.ds(pl.multiple_of(block * GROUP + i * TILE, TILE), TILE), :] = sums[i]
        return carry

    lax.fori_loop(0, blocks, one, 0)


def mix_backward_kernel(
    lead, groups, grad, source, taps_flipped, out, grad_taps, grad_f, rows_f, padded, table, sums_q
):
    blocks = source.shape[0] // GROUP
    tiles = GROUP // TILE
    top = LAGS // TILE - 1
    grad_f[...] = grad[...].astype(f32)
    rows_f[...] = source[...].astype(f32)
    padded[0:LAGS, :] = taps_flipped[...]
    padded[LAGS:, :] = jnp.zeros((TILE, padded.shape[1]), f32)
    for q in range(TILE):
        table[q] = padded[q : q + LAGS, :]
        sums_q[q] = jnp.zeros(sums_q.shape[1:], f32)

    def tile_of(ref, block, i):
        return ref[pl.ds(pl.multiple_of(block * GROUP + i * TILE, TILE), TILE), :]

    def add_to(q, tile, value):
        if isinstance(tile, int):
            place = slice(tile * TILE, (tile + 1) * TILE)
        else:
            place = pl.ds(pl.multiple_of(tile * TILE, TILE), TILE)
        sums_q[q, place, :] = sums_q[q, place, :] + value

    def one(block, carry):
        _, after = utterance_edges(groups, lead, blocks, block)
        sums = [jnp.zeros((TILE, rows_f.shape[1]), f32) for _ in range(tiles)]
        own = [tile_of(rows_f, block, j) for j in range(tiles)]
        here = [tile_of(grad_f, block, i) for i in range(tiles)]
        for q in range(TILE):
            lags = [lag_tile(table, TILE - 1 - q, top - d) for d in range(tiles)]
            for i in range(tiles):
                row = here[i][q : q + 1, :]
                for j in range(i + 1):
                    sums[j] = sums[j] + lags[i - j] * row
            rows = [own[j][q : q + 1, :] for j in range(tiles)]
            for d in range(tiles):
                total = here[d] * rows[0]
                for j in range(1, tiles - d):
                    total = total + here[d + j] * rows[j]
                add_to(q, d, total)

        def pair(other, sums):
            sums = list(sums)
            base = (other - block) * tiles
            here = [tile_of(grad_f, other, i) for i in range(tiles)]
            for q in range(TILE):
                lags = {
                    d: lag_tile(table, TILE - 1 - q, top - base - d)
                    for d in range(1 - tiles, tiles)
                }
                for i in range(tiles):
                    row = here[i][q : q + 1, :]
                    for j in range(tiles):
                        sums[j] = sums[j] + lags[i - j] * row
                rows = [own[j][q : q + 1, :] for j in range(tiles)]
                for d in range(1 - tiles, tiles):
                    total = None
                    for j in range(tiles):
                        if 0 <= j + d < tiles:
                            term = here[j + d] * rows[j]
                            total = term if total is None else total + term
                    add_to(q, base + d, total)
            return tuple(sums)

        sums = lax.fori_loop(block + 1, after, pair, tuple(sums))
        for j in range(tiles):
            out[pl.ds(pl.multiple_of(block * GROUP + j * TILE, TILE), TILE), :] = sums[j]
        return carry

    lax.fori_loop(0, blocks, one, 0)
    total = sums_q[0, 0:LAGS, :]
    for q in range(1, TILE):
        total = total + sums_q[q, q : q + LAGS, :]
    grad_taps[...] = total


def mixer_params():
    return pltpu.CompilerParams(vmem_limit_bytes=40 * 1024 * 1024)


def mix_forward(lead, groups, source, taps):
    rows, features = source.shape
    lanes = min(LANES, features)
    column = lambda count: pl.BlockSpec((count, lanes), lambda i: (0, i))
    return pl.pallas_call(
        partial(mix_forward_kernel, lead),
        out_shape=jax.ShapeDtypeStruct((rows, features), f32),
        grid=(features // lanes,),
        in_specs=[pl.BlockSpec(memory_space=pltpu.SMEM), column(rows), column(LAGS)],
        out_specs=column(rows),
        scratch_shapes=[
            pltpu.VMEM((rows, lanes), f32),
            pltpu.VMEM((LAGS + TILE, lanes), f32),
            pltpu.VMEM((TILE, LAGS, lanes), f32),
        ],
        compiler_params=mixer_params(),
        cost_estimate=pl.CostEstimate(
            flops=30000 * rows * features, bytes_accessed=rows * features * 8, transcendentals=0
        ),
        name="mix_forward",
    )(groups, source, taps)


def mix_backward(lead, groups, grad, source, taps_flipped, begin, width, into=None):
    rows, features = source.shape
    column = lambda count: pl.BlockSpec((count, width), lambda i: (0, begin))
    kept = [] if into is None else list(into)
    kernel = partial(mix_backward_kernel, lead)

    def body(*refs):
        kernel(*refs[:4], *refs[4 + len(kept) :])

    return pl.pallas_call(
        body,
        out_shape=(
            jax.ShapeDtypeStruct((rows, features), f32),
            jax.ShapeDtypeStruct((LAGS, features), f32),
        ),
        grid=(1,),
        in_specs=[
            pl.BlockSpec(memory_space=pltpu.SMEM),
            column(rows),
            column(rows),
            column(LAGS),
        ]
        + [pl.BlockSpec(memory_space=pl.ANY)] * len(kept),
        out_specs=(column(rows), column(LAGS)),
        scratch_shapes=[
            pltpu.VMEM((rows, width), f32),
            pltpu.VMEM((rows, width), f32),
            pltpu.VMEM((LAGS + TILE, width), f32),
            pltpu.VMEM((TILE, LAGS, width), f32),
            pltpu.VMEM((TILE, LAGS + TILE, width), f32),
        ],
        input_output_aliases={4 + i: i for i in range(len(kept))},
        compiler_params=mixer_params(),
        cost_estimate=pl.CostEstimate(
            flops=10000 * rows * width, bytes_accessed=rows * width * 8, transcendentals=0
        ),
        name="mix_backward",
    )(groups, grad, source, taps_flipped, *kept)


def fill_window(window, rows, before, after, lead, groups, block, blocks):
    first, stop = utterance_edges(groups, lead, blocks, block)
    place = lambda start, count: pl.ds(pl.multiple_of(start, 2 * TILE), count)
    window[TILE : TILE + GROUP, :] = rows[place(block * GROUP, GROUP), :].astype(f32)
    empty = jnp.zeros((TILE, window.shape[1]), f32)
    start = jnp.maximum(block * GROUP - 2 * TILE, 0)
    left = rows[place(start, 2 * TILE), :].astype(f32)[TILE:]
    left = jnp.where(block == 0, before[...].astype(f32), left)
    window[0:TILE, :] = jnp.where((block == 0) | (block > first), left, empty)
    start = jnp.minimum((block + 1) * GROUP, (blocks - 1) * GROUP)
    right = rows[place(start, 2 * TILE), :].astype(f32)[:TILE]
    right = jnp.where(block == lead - 1, after[...].astype(f32), right)
    keep = (block == lead - 1) | (block + 1 < stop)
    window[TILE + GROUP :, :] = jnp.where(keep, right, empty)


def conv_forward_kernel(lead, count, groups, rows, before, after, taps, out, window):
    blocks = rows.shape[0] // GROUP
    shift = TILE - count // 2

    def one(block, carry):
        fill_window(window, rows, before, after, lead, groups, block, blocks)
        total = None
        for k in range(count):
            term = window[shift + k : shift + k + GROUP, :] * taps[k : k + 1, :]
            total = term if total is None else total + term
        out[pl.ds(pl.multiple_of(block * GROUP, GROUP), GROUP), :] = total
        return carry

    lax.fori_loop(0, blocks, one, 0)


def conv_backward_kernel(
    lead, count, groups, grads, g_before, g_after, rows, before, after, taps, out, grad_taps,
    g_window, window, sums,
):
    blocks = rows.shape[0] // GROUP
    shift = TILE - count // 2
    sums[...] = jnp.zeros(sums.shape, f32)

    def one(block, carry):
        fill_window(g_window, grads, g_before, g_after, lead, groups, block, blocks)
        fill_window(window, rows, before, after, lead, groups, block, blocks)
        here = g_window[TILE : TILE + GROUP, :]
        total = None
        for k in range(count):
            lag = shift + count - 1 - k
            term = g_window[lag : lag + GROUP, :] * taps[k : k + 1, :]
            total = term if total is None else total + term
            product = here * window[shift + k : shift + k + GROUP, :]
            part = product[0:TILE]
            for i in range(TILE, GROUP, TILE):
                part = part + product[i : i + TILE]
            sums[k] = sums[k] + part
        out[pl.ds(pl.multiple_of(block * GROUP, GROUP), GROUP), :] = total
        return carry

    lax.fori_loop(0, blocks, one, 0)
    below = grad_taps.shape[0] - TILE - count
    grad_taps[...] = jnp.concatenate(
        [jnp.zeros((TILE, grad_taps.shape[1]), f32)]
        + [jnp.sum(sums[k], axis=0, keepdims=True) for k in range(count)]
        + [jnp.zeros((below, grad_taps.shape[1]), f32)],
        axis=0,
    )


def conv_call(kernel, lead, groups, arrays, outs, scratch, name):
    lanes = min(LANES, arrays[0].shape[1])
    column = lambda count: pl.BlockSpec((count, lanes), lambda i: (0, i))
    rows, features = arrays[0].shape
    return pl.pallas_call(
        kernel,
        out_shape=tuple(jax.ShapeDtypeStruct((n, features), f32) for n in outs),
        grid=(features // lanes,),
        in_specs=[pl.BlockSpec(memory_space=pltpu.SMEM)] + [column(a.shape[0]) for a in arrays],
        out_specs=tuple(column(n) for n in outs),
        scratch_shapes=[pltpu.VMEM(shape + (lanes,), f32) for shape in scratch],
        compiler_params=mixer_params(),
        cost_estimate=pl.CostEstimate(
            flops=4000 * rows * features, bytes_accessed=rows * features * 8, transcendentals=0
        ),
        name=name,
    )(groups, *arrays)


def conv_forward(lead, count, groups, rows, rim, taps):
    return conv_call(
        partial(conv_forward_kernel, lead, count),
        lead,
        groups,
        [rows, *rim, taps],
        [rows.shape[0]],
        [(GROUP + 2 * TILE,)],
        "conv_forward",
    )[0]


def conv_backward(lead, count, groups, grads, g_rim, rows, rim, taps):
    return conv_call(
        partial(conv_backward_kernel, lead, count),
        lead,
        groups,
        [grads, *g_rim, rows, *rim, taps],
        [rows.shape[0], SMALL_ROWS],
        [(GROUP + 2 * TILE,), (GROUP + 2 * TILE,), (count, TILE)],
        "conv_backward",
    )


def stack_rows(pieces, lanes):
    pieces = list(pieces)
    if any(p.shape[0] % 16 for p in pieces):
        fill = lambda p: jnp.pad(p, ((0, 0), (0, lanes - p.shape[1])))
        blocks = [b for p in pieces for b in (column_blocks(p, lanes) if p.shape[1] > lanes else [p])]
        return jnp.concatenate([fill(b) for b in blocks], axis=0)
    total = sum(p.shape[0] * -(-p.shape[1] // lanes) for p in pieces)

    def kernel(*refs):
        out, row = refs[-1], 0
        for ref in refs[:-1]:
            count, width = ref.shape
            for begin in range(0, width, lanes):
                here = min(lanes, width - begin)
                if here < lanes:
                    out[row : row + count, :] = jnp.zeros((count, lanes), out.dtype)
                out[row : row + count, 0:here] = ref[:, begin : begin + here]
                row += count

    return pl.pallas_call(
        kernel,
        out_shape=jax.ShapeDtypeStruct((total, lanes), pieces[0].dtype),
        in_specs=[pl.BlockSpec(memory_space=pltpu.VMEM)] * len(pieces),
        out_specs=pl.BlockSpec(memory_space=pltpu.VMEM),
        compiler_params=mixer_params(),
        name="stack_rows",
    )(*pieces)


def cmul(a, b):
    return (a[0] * b[0] - a[1] * b[1], a[0] * b[1] + a[1] * b[0])


def powers(rate, freq, steps):
    decay = jnp.exp(-rate * steps)
    return decay * jnp.cos(freq * steps), decay * jnp.sin(freq * steps)


def shifted(x, count):
    pad = jnp.zeros((abs(count),) + x.shape[1:], x.dtype)
    if count > 0:
        return jnp.concatenate([pad, x[:-count]], axis=0)
    return jnp.concatenate([x[-count:], pad], axis=0)


def chunk_scan(values, decay, sign):
    count = values[0].shape[0]
    hop = 1
    while hop < count:
        moved = tuple(shifted(v, sign * hop) for v in values)
        added = cmul(decay, moved)
        values = (values[0] + added[0], values[1] + added[1])
        decay = cmul(decay, decay)
        hop *= 2
    return values


def long_tables(log_rate, freq, coef, chunk):
    channels, states = log_rate.shape
    lanes = channels * states
    rate = jnp.exp(log_rate).reshape(1, lanes)
    freq = freq.reshape(1, lanes)
    scale = jnp.sqrt(2.0 * rate)
    weight = (
        scale * coef[:, :states].reshape(1, lanes),
        scale * coef[:, states:].reshape(1, lanes),
    )
    steps = jnp.arange(chunk + 1).astype(f32)[:, None]
    power = powers(rate, freq, steps)
    mask = jnp.arange(channels)[:, None] == (jnp.arange(lanes) // states)[None, :]
    mask = mask.astype(f32)[:, None, :]

    def spread(pair):
        wide = [(mask * part[None]).reshape(channels * chunk, lanes) for part in pair]
        return jnp.concatenate(wide, axis=1).astype(bf16)

    ages = tuple(p[:chunk][::-1] for p in power)
    leads = tuple(p[1:] for p in power)
    weighted = lambda pair: cmul(weight, pair)
    signed = lambda pair: (pair[0], -pair[1])
    return {
        "ages": spread(ages),
        "ages_slope": spread(tuple(a * steps[:chunk][::-1] for a in ages)),
        "leads": spread(leads),
        "leads_slope": spread(tuple(a * steps[1:] for a in leads)),
        "read": spread(signed(weighted(leads))),
        "read_back": spread(signed(weighted(ages))),
        "decay": powers(rate, freq, jnp.float32(chunk)),
        "rate": rate,
        "scale": scale,
        "weight": weight,
    }


def halves(x):
    lanes = x.shape[1] // 2
    return x[:, :lanes], x[:, lanes:]


def long_forward(rows, tables):
    added = halves(row_dot(rows, tables["ages"]))
    state = chunk_scan(added, tables["decay"], 1)
    before = tuple(shifted(v, 1) for v in state)
    carried = outer_dot(jnp.concatenate(before, axis=1).astype(bf16), tables["read"])
    return carried, before


def long_backward(grads, tables):
    read = halves(row_dot(grads, tables["leads"]))
    future = chunk_scan(read, tables["decay"], -1)
    later = tuple(shifted(v, -1) for v in future)
    return outer_dot(jnp.concatenate(later, axis=1).astype(bf16), tables["read_back"])


def long_moments(rows, grads, tables, before, chunk):
    added = halves(row_dot(rows, tables["ages_slope"]))
    late = cmul(tables["decay"], before)
    added = tuple(a + chunk * b for a, b in zip(added, late))
    slope_before = tuple(shifted(v, 1) for v in chunk_scan(added, tables["decay"], 1))
    read = halves(row_dot(grads, tables["leads"]))
    slope = halves(row_dot(grads, tables["leads_slope"]))
    total = lambda pair: tuple(jnp.sum(v, axis=0, keepdims=True) for v in pair)
    moment = total(cmul(read, before))
    first = cmul(slope, before)
    second = cmul(read, slope_before)
    return moment, total((first[0] + second[0], first[1] + second[1]))


def lag_values(log_rate, freq, coef, lags):
    states = log_rate.shape[1]
    rate = jnp.exp(log_rate)
    scale = jnp.sqrt(2.0 * rate)
    steps = jnp.arange(lags).astype(f32)
    real, imaginary = powers(rate[:, :, None], freq[:, :, None], steps)
    weights = (scale * coef[:, :states], scale * coef[:, states:])
    taps = jnp.sum(weights[0][:, :, None] * real - weights[1][:, :, None] * imaginary, axis=1)
    return taps, (real, imaginary)


def local(*args):
    Folding.last = None
    return layer(*args)


def layer(
    feats_long,
    feats_short,
    long_length,
    short_groups,
    freq_start,
    freq_width,
    time_start,
    time_width,
    stem_weight,
    norm_gains,
    ffn1_up,
    ffn1_down,
    mixer_in,
    mixer_out,
    mixer_log_rate,
    mixer_freq,
    mixer_coef,
    conv_taps,
    ffn2_up,
    ffn2_down,
    cotangent_long,
    cotangent_short,
):
    devices = lax.axis_size("tm") * lax.axis_size("head")
    own = stem_weight.shape[0]
    features = own * devices
    hidden_width = ffn1_up.shape[1]
    mel_bins = feats_long.shape[1]
    stem_width = stem_weight.shape[1]
    gain_count, tap_count = norm_gains.shape[1], conv_taps.shape[1]
    down_rows = ffn1_down.shape[0]
    up_blocks = hidden_width // features
    long_rows = feats_long.shape[0] // 4
    short_rows = feats_short.shape[0] // 4
    lead = long_rows // GROUP
    padded_to = lambda w, lanes: jnp.pad(w, ((0, 0), (0, lanes - w.shape[1])))

    block = stack_rows(
        [ffn1_up, mixer_in[:, :features], ffn1_down, stem_weight], features
    )
    split = own * (up_blocks + 1)
    got = [block] + [send_along_z(block, hops) for hops in range(1, grid_of()[0])]
    held = [
        stacked_along_z([g[:split] for g in got]),
        stacked_along_z([g[split:] for g in got]),
    ]
    back = stack_rows([ffn2_up, ffn2_down, mixer_out, mixer_in[:, features:]], features)

    held, mixer_params_own = tied(held, (mixer_log_rate, mixer_freq, mixer_coef))
    log_rate, freq_values, coef_values = (p.astype(f32) for p in mixer_params_own)
    own_taps, lag_powers = lag_values(log_rate, freq_values, coef_values, LAGS)
    shared = jnp.concatenate([own_taps.astype(bf16), norm_gains, conv_taps], axis=1)
    shared = padded_to(shared, -(-shared.shape[1] // 128) * 128)
    shared = exchange(jnp.broadcast_to(shared, (devices,) + shared.shape))

    dims = [[], []]
    orders = [bit_order("x"), bit_order("y")]
    tables_in = (log_rate, freq_values, coef_values)
    for step in range(len(orders[0])):
        for color in range(2):
            name = orders[color][step]
            other = swap(held[color], name)
            dims[color] = [n for n in places() if n in dims[color] or n == name]
            held[color] = joined_at(
                1 + dims[color].index(name), held[color], other, my_bit(name)
            )
        if step == 0:
            held, (tables_in, back) = tied(held, (tables_in, back))
    back_full = lax.all_gather(back, AXES, axis=0)
    mel_index = jnp.arange(mel_bins)
    mel_band = (mel_index >= freq_start[0]) & (mel_index < freq_start[0] + freq_width[0])
    freq_keep = (1 - mel_band.astype(jnp.int32)).astype(bf16)
    row_index = jnp.arange(4 * short_rows)
    time_blank = (row_index >= time_start[0]) & (row_index < time_start[0] + time_width[0])
    time_keep = (1 - time_blank.astype(jnp.int32)).astype(bf16)
    stacked = jnp.concatenate(
        [
            (feats_long * freq_keep[None, :]).reshape(long_rows, 4 * mel_bins),
            (feats_short * freq_keep[None, :] * time_keep[:, None]).reshape(
                short_rows, 4 * mel_bins
            ),
        ],
        axis=0,
    )
    stacked = padded_to(stacked, features)
    tables = long_tables(*tables_in, long_rows)
    shared = shared.reshape(features, -1).astype(f32).T
    held, (tables["ages"], shared, stacked) = tied(held, (tables["ages"], shared, stacked))
    core = ("head", 0)
    other = [swap(h, core) for h in held]

    def assembled(color, begin, count, lanes=features):
        part = lambda v: v[..., begin : begin + count, :lanes]
        full = joined_at(1 + len(dims[color]), part(held[color]), part(other[color]), my_bit(core))
        return full.reshape(-1, lanes)

    up_first = [assembled(0, i * own, own) for i in range(up_blocks)]
    proj_inner = assembled(0, up_blocks * own, own)
    down_first = assembled(1, 0, down_rows)
    stem_full = assembled(1, down_rows, own)

    lag_taps = shared[:LAGS]
    lag_flipped = lag_taps[::-1]
    gains = shared[LAGS : LAGS + gain_count]
    taps = padded_to(shared[LAGS + gain_count : LAGS + gain_count + tap_count].T, 16).T

    position = lax.axis_index(AXES) * long_rows + jnp.arange(long_rows)
    valid_long = (position < long_length[0]).astype(f32)
    valid = jnp.concatenate([valid_long, jnp.ones((short_rows,), f32)])[:, None]
    valid_b = valid.astype(bf16)

    residual = outer_dot(stacked, stem_full)
    ffn_first, kept_first = ffn_forward(residual, gains[0], up_first, down_first)
    residual1 = residual + 0.5 * ffn_first
    hat2, scale2 = norm(residual1)
    normed2 = (hat2 * gains[1]).astype(bf16)
    inputs_b = row_dot(normed2, proj_inner).astype(bf16)
    source_b = inputs_b * valid_b

    def to_owner(rows):
        return rows.T.reshape(devices, 8, own * long_rows // 8)

    def at_owner(rows):
        return exchange(rows).reshape(devices, own * long_rows)

    def from_owner(rows):
        return exchange(rows.astype(bf16).reshape(devices, 8, own * long_rows // 8))

    def at_home(rows):
        return rows.reshape(features, long_rows).T.astype(f32)

    long_in, normed2 = tied(to_owner(source_b[:long_rows]), normed2)
    long_in = at_owner(long_in)
    carried, before = long_forward(long_in, tables)
    carried, source_b = tied(carried.astype(bf16), source_b)
    carried = from_owner(carried)
    mixed = mix_forward(lead, short_groups, source_b, lag_taps)
    up_second = [
        back_full[:, i : i + own].reshape(features, features)
        for i in range(0, own * up_blocks, own)
    ]
    place = own * up_blocks
    down_second = back_full[:, place : place + down_rows].reshape(hidden_width, features)
    place += down_rows
    proj_out = back_full[:, place : place + own].reshape(features, features)
    proj_gate = back_full[:, place + own :].reshape(features, features)
    gates = row_dot(normed2, proj_gate)
    gate_act = jax.nn.silu(gates)

    below = lambda v: jnp.pad(v, ((0, short_rows), (0, 0)))
    mixed = (mixed + below(at_home(carried))).astype(bf16).astype(f32)
    inputs_f = inputs_b.astype(f32)
    joined = mixed + gains[5] * inputs_f
    gated_b = (joined * gate_act).astype(bf16)

    residual2 = residual1 + row_dot(gated_b, proj_out)
    hat3, scale3 = norm(residual2)
    spread_b = (hat3 * gains[2]).astype(bf16) * valid_b
    rim = edges(spread_b[:long_rows], TILE)
    pre = conv_forward(lead, tap_count, short_groups, spread_b, rim, taps)
    residual3 = residual2 + jax.nn.silu(pre)
    ffn_second, kept_second = ffn_forward(residual3, gains[3], up_second, down_second)
    residual4 = residual3 + 0.5 * ffn_second
    hat5, scale5 = norm(residual4)
    final = (hat5 * gains[4]).astype(bf16)

    cotangent = jnp.concatenate([cotangent_long, cotangent_short], axis=0).astype(f32)
    grad4, grad_gain4 = norm_back(cotangent, gains[4], hat5, scale5)
    grad_b = (0.5 * grad4).astype(bf16)
    grad_hidden = hidden_grad(grad_b, kept_second, down_second)
    normed, _, active, hat, scale = kept_second
    by_owner = lambda g: g.astype(bf16).reshape(devices, -1, g.shape[1])
    piece, grad_gain3 = norm_back(back_through(grad_hidden, up_second), gains[3], hat, scale)
    grad3 = grad4 + piece
    grad_pre_b = (grad3 * silu_slope(pre)).astype(bf16)
    grad_pre_b, (normed, active) = tied(grad_pre_b, (normed, active))
    grad_rim = edges(grad_pre_b[:long_rows], TILE)
    second = Folding(
        [by_owner(inner_dot(normed, grad_hidden)), by_owner(inner_dot(active, grad_b))]
    )
    grad_pre_b = advance([second], grad_pre_b)
    grad_spread, small_rows = conv_backward(
        lead, tap_count, short_groups, grad_pre_b, grad_rim, spread_b, rim, taps
    )
    piece, grad_gain2 = norm_back(grad_spread * valid, gains[2], hat3, scale3)
    grad2 = grad3 + piece
    grad_out_b = advance([second], grad2.astype(bf16))
    grad_gated = outer_dot(grad_out_b, proj_out)
    grad_joined = grad_gated * gate_act
    grad_mixed_b = grad_joined.astype(bf16)
    grad_in, (grad_mixed_b, gated_b) = tied(
        to_owner(grad_mixed_b[:long_rows]), (grad_mixed_b, gated_b)
    )
    grad_in = at_owner(grad_in)
    grad_gates = grad_gated * joined * silu_slope(gates)
    grad_gain5 = jnp.sum(grad_joined * inputs_f, axis=0)
    grad_proj_out = by_owner(inner_dot(gated_b, grad_out_b))
    half = features // 2
    run = lambda grad, begin, into=None: mix_backward(
        lead, short_groups, grad, source_b, lag_flipped, begin, half, into
    )
    first_half = run(grad_mixed_b, 0)
    later = long_backward(grad_in, tables)
    later, grad_mixed_b = tied(later.astype(bf16), grad_mixed_b)
    later = from_owner(later)
    grad_mixed_b = advance([second], grad_mixed_b)
    grad_source, grad_lags = run(grad_mixed_b, 1, first_half)
    grad_source = (grad_source + below(at_home(later))).astype(bf16).astype(f32)
    grad_inner_b = (grad_source * valid + gains[5] * grad_joined).astype(bf16)
    grad_inner_b = advance([second], grad_inner_b)
    grad_gates_b = grad_gates.astype(bf16)
    back = outer_dot(grad_inner_b, proj_inner) + outer_dot(grad_gates_b, proj_gate)
    piece, grad_gain1 = norm_back(back, gains[1], hat2, scale2)
    grad1 = grad2 + piece
    grad_b = (0.5 * grad1).astype(bf16)
    normed, _, active, hat, scale = kept_first
    unit = (jnp.arange(LAGS)[:, None] == jnp.arange(features)[None, :]).astype(bf16)
    early_out = jnp.concatenate(
        [
            by_owner(inner_dot(normed2, grad_inner_b)),
            by_owner(inner_dot(normed2, grad_gates_b)),
            grad_proj_out,
            by_owner(inner_dot(grad_lags.astype(bf16), unit)),
        ],
        axis=1,
    )
    early = Folding([by_owner(inner_dot(active, grad_b)), early_out], 0)
    grad_b = advance([early], grad_b)
    grad_hidden = hidden_grad(grad_b, kept_first, down_first)
    grad_hidden = advance([second], grad_hidden)
    late = Folding([by_owner(inner_dot(normed, grad_hidden))], 0)
    grad_hidden = advance([late, early], grad_hidden)
    piece, grad_gain0 = norm_back(back_through(grad_hidden, up_first), gains[0], hat, scale)
    grad_zero_b = settle(second, advance([late], (grad1 + piece).astype(bf16)))

    row = jnp.arange(SMALL_ROWS)[:, None]
    gain_rows = [grad_gain0, grad_gain1, grad_gain2, grad_gain3, grad_gain4, grad_gain5]
    for k, grad_gain in enumerate(gain_rows):
        small_rows = jnp.where(row == k, grad_gain[None, :], small_rows)
    lane = jnp.arange(features)[None, :] - stem_width
    place = jnp.where(lane < gain_count, lane, lane - gain_count + TILE)
    small_unit = ((place == row) & (lane >= 0) & (lane < gain_count + tap_count)).astype(bf16)
    small_lanes = -(-(stem_width + gain_count + tap_count) // 128) * 128
    small = inner_dot(grad_zero_b, stacked) + inner_dot(small_rows.astype(bf16), small_unit)
    small = exchange(by_owner(small[:, :small_lanes]))
    grad_zero_b = advance([early], grad_zero_b)
    grad_stacked = row_dot(grad_zero_b, stem_full)[:, :stem_width]
    freq_float = freq_keep.astype(f32)
    time_float = time_keep.astype(f32)
    input_long = (
        grad_stacked[:long_rows].reshape(4 * long_rows, mel_bins) * freq_float[None, :]
    ).astype(bf16)
    input_short = (
        grad_stacked[long_rows:].reshape(4 * short_rows, mel_bins)
        * freq_float[None, :]
        * time_float[:, None]
    ).astype(bf16)
    while not second.done:
        advance([second])
    sum_up2, sum_down2 = second.result()
    hold(late, (sum_up2, sum_down2))
    input_long, input_short = advance([late], (input_long, input_short))
    moment_in = (long_in, grad_in, before)
    while not early.done:
        moment_in = advance([early], moment_in)
    moment, moment_slope = long_moments(*moment_in[:2], tables, moment_in[2], long_rows)
    early.got = advance([late], early.got)
    early.got = tied((moment, moment_slope), early.got)[1]
    sum_early = early.result()
    grad_small = jnp.sum(small.astype(f32), axis=0)
    (sum_up1,) = late.result()
    sum_down1, rest = sum_early
    sum_in = jnp.concatenate([rest[:own], rest[own : 2 * own]], axis=1)
    sum_out = rest[2 * own : 3 * own]
    lag_grad = rest[3 * own :, :LAGS]

    states = log_rate.shape[1]
    steps = jnp.arange(LAGS).astype(f32)
    near = tuple(jnp.sum(lag_grad[:, None, :] * p, axis=2) for p in lag_powers)
    near_slope = tuple(jnp.sum((lag_grad * steps)[:, None, :] * p, axis=2) for p in lag_powers)
    shape = (own, states)
    moment = tuple(a.reshape(shape) + b for a, b in zip(moment, near))
    moment_slope = tuple(a.reshape(shape) + b for a, b in zip(moment_slope, near_slope))
    weight = tuple(w.reshape(shape) for w in tables["weight"])
    rate = tables["rate"].reshape(shape)
    scale = tables["scale"].reshape(shape)
    pulled = cmul(weight, moment)
    pulled_slope = cmul(weight, moment_slope)
    grad_rate = 0.5 * pulled[0] - rate * pulled_slope[0]
    grad_freq = -pulled_slope[1]
    grad_coef = jnp.concatenate([scale * moment[0], -scale * moment[1]], axis=1)

    return (
        final[:long_rows],
        final[long_rows:],
        input_long,
        input_short,
        grad_small[:, :stem_width],
        grad_small[:, stem_width : stem_width + gain_count],
        sum_up1,
        sum_down1,
        sum_in,
        sum_out,
        grad_rate,
        grad_freq,
        grad_coef,
        grad_small[:, stem_width + gain_count : stem_width + gain_count + tap_count],
        sum_up2,
        sum_down2,
    )


def solution(mesh):
    rows = P(AXES, None)
    flat = P(AXES)
    return jax.shard_map(
        local,
        mesh=mesh,
        in_specs=(rows, rows, P(), rows, flat, flat, flat, flat) + (rows,) * 14,
        out_specs=(rows,) * 16,
        check_vma=False,
    )
```
